256 devices in a mesh: dp: 16 (over z_lo, y, core), space: 16 (over x, z_hi).
Axes of the slice: x: 4, y: 4, z: 8 (z_hi: 4, z_lo: 2; z = z_hi * 2 + z_lo), core: 2. Of those that a mesh axis runs over, the one named last changes fastest.
Arguments:
- cotangent: bfloat16 [16, 96, 368, 768], P('dp', None, 'space'), may hold values from -6 to 6
- spectrum: bfloat16 [16, 2, 96, 368, 368], P('dp', None, None, 'space'), may hold values from -6 to 6
- first_weight: bfloat16 [2, 1, 96, 96], replicated, may hold values from -0.4375 to 0.4375
- first_bias: bfloat16 [2, 1, 96], replicated, may hold values from -3 to 3
- second_weight: bfloat16 [2, 1, 96, 96], replicated, may hold values from -0.4375 to 0.4375
- second_bias: bfloat16 [2, 1, 96], replicated, may hold values from -3 to 3
Outputs:
- grad_input: bfloat16 [16, 96, 368, 768], P('dp', None, 'space')
- grad_first_weight: float32 [2, 1, 96, 96], P(None, None, 'dp')
- grad_first_bias: float32 [2, 1, 96], P(None, None, 'dp')
- grad_second_weight: float32 [2, 1, 96, 96], P(None, None, 'dp')
- grad_second_bias: float32 [2, 1, 96], P(None, None, 'dp')
The draws below stay inside these ranges and needn't reach their ends.
All inputs are finite; a program needn't handle non-finite values.
Results may differ from the reference program's by a relative error of at most 0.011.
The reference program's roundings to bfloat16 on the way count: a program that leaves them out, or rounds other values in their place, can miss the bound.
Values may be sent and summed in bfloat16 or wider, within the bound.
A program may use at most 128 MiB of HBM per device.

```python
import math
import jax
import jax.numpy as jnp
from jax import lax

H = 368
W = 768
KW = 368
BS = 96
BLOCKS = 1
C = 96
SAMPLES = 16


def shard_levels(stream_key, extent, cuts, smallest, high):
    level, own = 1.0, jax.random.fold_in(stream_key, 6)
    for axis_at, blocks in cuts:
        steps = jnp.exp(jax.random.uniform(jax.random.fold_in(own, axis_at), (blocks,), jnp.float32, smallest / len(cuts), high / len(cuts)))
        level = level * jnp.repeat(steps, extent[axis_at] // blocks).reshape([-1 if axis == axis_at else 1 for axis in range(len(extent))])
    return level


def normal_values(own_key, dims, deviation, reach, split=(), kind=jnp.bfloat16):
    gain = shard_levels(own_key, dims, split, -0.22, 0.18) if split else 1.0
    entries = jax.random.normal(own_key, dims, jnp.float32) * deviation * gain
    return jnp.minimum(jnp.maximum(entries, -reach), reach).astype(kind)


def setup_inputs(seed: int = 0) -> dict:
    keys = jax.random.split(jax.random.key(seed), 7)
    return {
        "cotangent": normal_values(keys[0], (SAMPLES, C, H, W), 1.0, 6.0, ((0, 16), (2, 16))),
        "spectrum": normal_values(keys[1], (SAMPLES, 2, C, KW, H), 1.0, 6.0, ((0, 16), (3, 16))),
        "first_weight": normal_values(keys[2], (2, BLOCKS, BS, BS), (2 * BS) ** -0.5, 0.4375),
        "first_bias": normal_values(keys[3], (2, BLOCKS, BS), 0.5, 3.0),
        "second_weight": normal_values(keys[4], (2, BLOCKS, BS, BS), (2 * BS) ** -0.5, 0.4375),
        "second_bias": normal_values(keys[5], (2, BLOCKS, BS), 0.5, 3.0),
    }


def angle_tables(n, rows, cols):
    index = jnp.arange(rows, dtype=jnp.int32)[:, None] * jnp.arange(cols, dtype=jnp.int32)[None, :] % n
    theta = index.astype(jnp.float32) * (2.0 * math.pi / n)
    return (jnp.cos(theta).astype(jnp.bfloat16), jnp.sin(theta).astype(jnp.bfloat16))

def rounded(value):
    return lax.optimization_barrier(value.astype(jnp.bfloat16)).astype(jnp.float32)

def mix_fwd(inputs, weight):
    return jnp.einsum('bckp,bcd->bdkp', inputs, weight)

def mix_back(inputs, weight):
    return jnp.einsum('bdkp,bcd->bckp', inputs, weight)

def outer_sum(left, right):
    return jnp.einsum('bckp,bdkp->bcd', left, right)

def one_sample(grad_out, saved, first_weight, first_bias, second_weight, second_bias):
    lon_cos, lon_sin = angle_tables(W, W, KW)
    lat_cos, lat_sin = angle_tables(H, H, H)
    lon_cos = lon_cos.astype(jnp.float32)
    lon_sin = lon_sin.astype(jnp.float32)
    lat_cos = lat_cos.astype(jnp.float32)
    lat_sin = lat_sin.astype(jnp.float32)
    scale = 1.0 / math.sqrt(H * W)
    mult = jnp.where(jnp.arange(KW) == 0, 1.0, 2.0).astype(jnp.float32) * scale
    grad_f = grad_out.astype(jnp.float32)
    lon_re = rounded(jnp.einsum('chw,wk->ckh', grad_f, lon_cos))
    lon_im = rounded(-jnp.einsum('chw,wk->ckh', grad_f, lon_sin))
    dz_re = (jnp.einsum('ckh,hp->ckp', lon_re, lat_cos) + jnp.einsum('ckh,hp->ckp', lon_im, lat_sin)) * mult[None, :, None]
    dz_im = (jnp.einsum('ckh,hp->ckp', lon_im, lat_cos) - jnp.einsum('ckh,hp->ckp', lon_re, lat_sin)) * mult[None, :, None]
    dz_re = dz_re.reshape(BLOCKS, BS, KW, H)
    dz_im = dz_im.reshape(BLOCKS, BS, KW, H)
    y_all = saved.astype(jnp.float32).reshape(2, BLOCKS, BS, KW, H)
    y_re, y_im = (y_all[0], y_all[1])
    w1r = first_weight[0].astype(jnp.float32)
    w1i = first_weight[1].astype(jnp.float32)
    w2r = second_weight[0].astype(jnp.float32)
    w2i = second_weight[1].astype(jnp.float32)
    b1 = first_bias.astype(jnp.float32)[:, :, :, None, None]
    b2 = second_bias.astype(jnp.float32)[:, :, :, None, None]
    u_re = mix_fwd(y_re, w1r) - mix_fwd(y_im, w1i) + b1[0]
    u_im = mix_fwd(y_re, w1i) + mix_fwd(y_im, w1r) + b1[1]
    a_re = rounded(jnp.maximum(u_re, 0.0))
    a_im = rounded(jnp.maximum(u_im, 0.0))
    v_re = mix_fwd(a_re, w2r) - mix_fwd(a_im, w2i) + b2[0]
    v_im = mix_fwd(a_re, w2i) + mix_fwd(a_im, w2r) + b2[1]
    dv_re = rounded(jnp.where(jnp.abs(v_re) > 0.01, dz_re, 0.0))
    dv_im = rounded(jnp.where(jnp.abs(v_im) > 0.01, dz_im, 0.0))
    gw2 = jnp.stack([outer_sum(a_re, dv_re) + outer_sum(a_im, dv_im), outer_sum(a_re, dv_im) - outer_sum(a_im, dv_re)])
    gb2 = jnp.stack([lax.optimization_barrier(jnp.sum(dv_re, axis=(2, 3))), lax.optimization_barrier(jnp.sum(dv_im, axis=(2, 3)))])
    da_re = mix_back(dv_re, w2r) + mix_back(dv_im, w2i)
    da_im = mix_back(dv_im, w2r) - mix_back(dv_re, w2i)
    du_re = rounded(jnp.where(u_re > 0.0, da_re, 0.0))
    du_im = rounded(jnp.where(u_im > 0.0, da_im, 0.0))
    gw1 = jnp.stack([outer_sum(y_re, du_re) + outer_sum(y_im, du_im), outer_sum(y_re, du_im) - outer_sum(y_im, du_re)])
    gb1 = jnp.stack([lax.optimization_barrier(jnp.sum(du_re, axis=(2, 3))), lax.optimization_barrier(jnp.sum(du_im, axis=(2, 3)))])
    dy_re = rounded(mix_back(du_re, w1r) + mix_back(du_im, w1i)).reshape(C, KW, H)
    dy_im = rounded(mix_back(du_im, w1r) - mix_back(du_re, w1i)).reshape(C, KW, H)
    q_re = rounded(jnp.einsum('ckp,ph->ckh', dy_re, lat_cos) - jnp.einsum('ckp,ph->ckh', dy_im, lat_sin))
    q_im = rounded(jnp.einsum('ckp,ph->ckh', dy_re, lat_sin) + jnp.einsum('ckp,ph->ckh', dy_im, lat_cos))
    back = jnp.einsum('ckh,wk->chw', q_re, lon_cos) - jnp.einsum('ckh,wk->chw', q_im, lon_sin)
    grad_in = (grad_f + scale * back).astype(jnp.bfloat16)
    return (grad_in, gw1, gb1, gw2, gb2)

def reference(cotangent, spectrum, first_weight, first_bias, second_weight, second_bias):

    def per_sample(pair):
        return one_sample(pair[0], pair[1], first_weight, first_bias, second_weight, second_bias)
    grad_in, gw1, gb1, gw2, gb2 = lax.map(per_sample, (cotangent, spectrum))
    return (grad_in, lax.optimization_barrier(jnp.sum(gw1, axis=0)), lax.optimization_barrier(jnp.sum(gb1, axis=0)), lax.optimization_barrier(jnp.sum(gw2, axis=0)), lax.optimization_barrier(jnp.sum(gb2, axis=0)))
```

```python
import math

import jax
import jax.numpy as jnp
import ml_dtypes
import numpy as np
from jax import lax
from jax.experimental import pallas as pl
from jax.experimental.pallas import tpu as pltpu
from jax.sharding import PartitionSpec as P

H = 368
W = 768
KW = 368
C = 96
G = 16
HL = 23
HP = 24
CP = 128
CH = 3
KC = 8
ROWS = G * 2 * KC
MSG = 2 * HP
PP = 384
SCALE = 1.0 / math.sqrt(H * W)
LAM = 0.01
F32 = jnp.float32
BF16 = jnp.bfloat16
MESH = pl.DeviceIdType.MESH


def angles(n, rows, cols):
    index = (rows[:, None].astype(np.int64) * cols[None, :].astype(np.int64)) % n
    theta = index.astype(np.float32) * np.float32(2.0 * math.pi / n)
    return np.cos(theta), np.sin(theta)


def lon_table():
    cos, sin = angles(W, np.arange(KW), np.arange(W))
    both = np.stack([cos, -sin], 1).reshape(G, HL, 2, W)
    full = np.zeros((G, CH * KC, 2, W), np.float32)
    full[:, :HL] = both
    full = full.reshape(G, CH, KC, 2, W).transpose(1, 0, 3, 2, 4)
    return full.reshape(CH, ROWS, W).astype(ml_dtypes.bfloat16)


def lat_table():
    cos, sin = angles(H, np.arange(H), np.arange(H))
    full = np.zeros((G, 2, HP, 2, PP), np.float32)
    cos, sin = cos.reshape(G, HL, H), sin.reshape(G, HL, H)
    full[:, 0, :HL, 0, :H] = cos
    full[:, 1, :HL, 0, :H] = sin
    full[:, 0, :HL, 1, :H] = -sin
    full[:, 1, :HL, 1, :H] = cos
    return full.reshape(G * MSG, 2 * PP).astype(ml_dtypes.bfloat16)


def nt(a, b):
    return lax.dot_general(a, b, (((1,), (1,)), ((), ())), preferred_element_type=F32)


def tn(a, b):
    return lax.dot_general(a, b, (((0,), (0,)), ((), ())), preferred_element_type=F32)


def nn(a, b):
    return jnp.dot(a, b, preferred_element_type=F32)


def kernel(
    x_hbm, y_hbm, lon_hbm, lat_hbm, w1t_ref, w1_ref, w2t_ref, w2_ref, b1_ref, b2_ref,
    out_ref, g_ref,
    x_ref, y_ref, lon_ref, lat_ref, fs, fr, bs, br, work, acc, dy_ref, gw1, gw2, gb1, gb2, gs, gr, hs, hr,
    load_sem, fs_sem, fr_sem, bs_sem, br_sem, gs_sem, gr_sem, hs_sem, hr_sem,
):
    me = lax.axis_index("space")
    row = lax.axis_index("dp")

    barrier = pltpu.get_barrier_semaphore()

    def greet(o, carry):
        pl.semaphore_signal(
            barrier, inc=1, device_id={"space": lax.rem(me + o, G)}, device_id_type=MESH
        )
        pl.semaphore_signal(
            barrier, inc=1, device_id={"dp": lax.rem(row + o, G)}, device_id_type=MESH
        )
        return carry

    lax.fori_loop(1, G, greet, 0)
    loads = [
        pltpu.make_async_copy(src, dst, load_sem.at[i])
        for i, (src, dst) in enumerate(
            [(lon_hbm, lon_ref), (x_hbm, x_ref), (lat_hbm, lat_ref), (y_hbm, y_ref)]
        )
    ]
    for load in loads:
        load.start()
    loads[0].wait()
    loads[1].wait()

    lane = lax.broadcasted_iota(jnp.int32, (HP, CP), 1)

    def longitude(j):
        def two(i, carry):
            pair = x_ref[pl.ds(2 * i, 2)].reshape(2 * CP, W)
            got = nt(lon_ref[j], pair)
            work[pl.ds(pl.multiple_of(2 * i * ROWS, ROWS), ROWS), :] = got[:, :CP]
            work[pl.ds(pl.multiple_of((2 * i + 1) * ROWS, ROWS), ROWS), :] = got[:, CP:]
            return carry

        lax.fori_loop(0, HP // 2, two, 0)

    def packed(owner):
        parts = []
        for half in range(KC // 4):
            rows = []
            for s in range(2):
                a = [
                    work[pl.ds(owner * 2 * KC + s * KC + half * 4 + k, HP, stride=ROWS), :]
                    for k in range(4)
                ]
                r1 = pltpu.roll(a[1], 96, 1)
                r2 = pltpu.roll(a[2], 64, 1)
                r3 = pltpu.roll(a[3], 32, 1)
                rows.append(
                    [
                        jnp.where(lane < 96, a[0], r1),
                        jnp.where(lane < 64, r1, r2),
                        jnp.where(lane < 32, r2, r3),
                    ]
                )
            for t in range(3):
                parts.append(jnp.concatenate([rows[0][t], rows[1][t]], 0).astype(BF16))
        return parts

    def forward_copy(j, peer):
        return pltpu.make_async_remote_copy(
            src_ref=fs.at[j, peer], dst_ref=fr.at[j, me], send_sem=fs_sem.at[j, peer],
            recv_sem=fr_sem.at[j, me], device_id={"space": peer}, device_id_type=MESH,
        )

    def forward_arrival(j, peer):
        return pltpu.make_async_remote_copy(
            src_ref=fs.at[j, peer], dst_ref=fr.at[j, peer], send_sem=fs_sem.at[j, peer],
            recv_sem=fr_sem.at[j, peer], device_id={"space": peer}, device_id_type=MESH,
        )

    def back_copy(j, peer):
        return pltpu.make_async_remote_copy(
            src_ref=bs.at[j, peer], dst_ref=br.at[j, me], send_sem=bs_sem.at[j, peer],
            recv_sem=br_sem.at[j, me], device_id={"space": peer}, device_id_type=MESH,
        )

    def back_arrival(j, peer):
        return pltpu.make_async_remote_copy(
            src_ref=bs.at[j, peer], dst_ref=br.at[j, peer], send_sem=bs_sem.at[j, peer],
            recv_sem=br_sem.at[j, peer], device_id={"space": peer}, device_id_type=MESH,
        )

    def send_chunk(j, carry):
        longitude(j)

        @pl.when(j == 0)
        def _():
            pl.semaphore_wait(barrier, 2 * (G - 1))

        def one(o, c):
            peer = lax.rem(me + o, G)
            for t, part in enumerate(packed(peer)):
                fs[j, peer, :, t * CP : (t + 1) * CP] = part
            forward_copy(j, peer).start()
            return c

        lax.fori_loop(1, G, one, 0)
        for t, part in enumerate(packed(me)):
            fr[j, me, :, t * CP : (t + 1) * CP] = part
        return carry

    lax.fori_loop(0, CH, send_chunk, 0)
    loads[2].wait()
    loads[3].wait()

    gw1[...] = jnp.zeros_like(gw1)
    gw2[...] = jnp.zeros_like(gw2)
    gb1[...] = jnp.zeros_like(gb1)
    gb2[...] = jnp.zeros_like(gb2)

    def folded(v):
        v = v.astype(F32)
        return v[:, :CP] + v[:, CP : 2 * CP] + v[:, 2 * CP :]

    def middle(j, carry):
        def arrive(o, c):
            forward_arrival(j, lax.rem(me + o, G)).wait_recv()
            return c

        lax.fori_loop(1, G, arrive, 0)
        for half in range(KC // 4):
            lanes = slice(half * PP, (half + 1) * PP)
            got = fr[j, :, :, lanes].reshape(G * MSG, PP)
            dz = tn(got, lat_ref[...])
            for k in range(4):
                at = j * KC + half * 4 + k
                mult = jnp.where(at + me == 0, SCALE, 2.0 * SCALE).astype(F32)
                dzk = dz[k * C : (k + 1) * C]
                dzk = jnp.concatenate([dzk[:, :PP], dzk[:, PP:]], 0) * mult
                yk = y_ref[at]
                u = nn(w1t_ref[...], yk) + b1_ref[...]
                a = jnp.maximum(u, 0.0).astype(BF16)
                v = nn(w2t_ref[...], a) + b2_ref[...]
                dv = jnp.where(jnp.abs(v) > LAM, dzk, 0.0).astype(BF16)
                gw2[...] += nt(a, dv)
                gb2[...] += folded(dv)
                da = nn(w2_ref[...], dv)
                du = jnp.where(u > 0.0, da, 0.0).astype(BF16)
                gw1[...] += nt(yk, du)
                gb1[...] += folded(du)
                dy = nn(w1_ref[...], du).astype(BF16)
                dy_ref[k * C : (k + 1) * C, :PP] = dy[:C]
                dy_ref[k * C : (k + 1) * C, PP:] = dy[C:]
            q = nt(lat_ref[...], dy_ref[...]).astype(BF16)
            bs[j, :, :, lanes] = q.reshape(G, MSG, PP)

        def one(o, c):
            back_copy(j, lax.rem(me + o, G)).start()
            return c

        lax.fori_loop(1, G, one, 0)
        br[j, me] = bs[j, me]
        return carry

    lax.fori_loop(0, CH, middle, 0)

    def combined(g):
        re = g[:C, :C] + g[C:, C:]
        im = g[:C, C:] - g[C:, :C]
        return re, im

    sums = []
    for g, b in ((gw1, gb1), (gw2, gb2)):
        total = jnp.sum(b[...], axis=1, keepdims=True)
        for part, bias in zip(combined(g[...]), (total[:C], total[C:])):
            wide = jnp.concatenate([part, jnp.broadcast_to(bias, (C, CP - C))], 1)
            sums.append(wide)
    for d in range(G):
        gs[d] = jnp.concatenate([s[6 * d : 6 * d + 6] for s in sums], 0)

    def grad_copy(peer, at):
        return pltpu.make_async_remote_copy(
            src_ref=gs.at[peer], dst_ref=gr.at[at], send_sem=gs_sem.at[peer],
            recv_sem=gr_sem.at[at], device_id={"dp": peer}, device_id_type=MESH,
        )

    def share_copy(peer, at):
        return pltpu.make_async_remote_copy(
            src_ref=hs, dst_ref=hr.at[at], send_sem=hs_sem.at[peer],
            recv_sem=hr_sem.at[at], device_id={"space": peer}, device_id_type=MESH,
        )

    def over_peers(first, body):
        def step(o, c):
            body(lax.rem(first + o, G))
            return c

        lax.fori_loop(1, G, step, 0)

    over_peers(row, lambda peer: grad_copy(peer, row).start())

    def finish(j):
        over_peers(me, lambda peer: back_arrival(j, peer).wait_recv())

        def unpack(g, c):
            for half in range(KC // 4):
                got = br[j, g, :, half * PP : (half + 1) * PP].astype(F32)
                for s in range(2):
                    p = [got[s * HP : (s + 1) * HP, t * CP : (t + 1) * CP] for t in range(3)]
                    parts = [
                        p[0],
                        jnp.where(lane < 32, pltpu.roll(p[0], 32, 1), pltpu.roll(p[1], 32, 1)),
                        jnp.where(lane < 64, pltpu.roll(p[1], 64, 1), pltpu.roll(p[2], 64, 1)),
                        pltpu.roll(p[2], 96, 1),
                    ]
                    for k in range(4):
                        at = g * 2 * KC + s * KC + half * 4 + k
                        work[pl.ds(at, HP, stride=ROWS), :] = parts[k]
            return c

        lax.fori_loop(0, G, unpack, 0)

        def one(h, c):
            q = work[pl.ds(pl.multiple_of(h * ROWS, ROWS), ROWS), :].astype(BF16)
            new = tn(q, lon_ref[j])[:C]
            if j == 0:
                acc[h] = new
            elif j < CH - 1:
                acc[h] += new
            else:
                total = x_ref[h, :C].astype(F32) + SCALE * (acc[h] + new)
                out_ref[h] = total.astype(BF16)
            return c

        lax.fori_loop(0, HL, one, 0)

    finish(0)
    over_peers(row, lambda peer: grad_copy(peer, peer).wait_recv())
    gr[row] = gs[row]
    hs[...] = jnp.sum(gr[...], axis=0)
    over_peers(me, lambda peer: share_copy(peer, me).start())
    finish(1)
    finish(2)
    over_peers(me, lambda peer: share_copy(peer, peer).wait_recv())
    hr[me] = hs[...]
    g_ref[...] = jnp.sum(hr[...], axis=0)

    for j in range(CH):
        over_peers(me, lambda peer, j=j: forward_copy(j, peer).wait_send())
        over_peers(me, lambda peer, j=j: back_copy(j, peer).wait_send())
    over_peers(row, lambda peer: grad_copy(peer, row).wait_send())
    over_peers(me, lambda peer: share_copy(peer, me).wait_send())


def complex_matrix(w):
    return jnp.concatenate(
        [jnp.concatenate([w[0], w[1]], 1), jnp.concatenate([-w[1], w[0]], 1)], 0
    )


def on_device(cotangent, spectrum, first_weight, first_bias, second_weight, second_bias):
    x = jnp.transpose(cotangent[0], (1, 0, 2))
    x = jnp.pad(x, ((0, HP - HL), (0, CP - C), (0, 0)))
    y = jnp.transpose(spectrum[0], (2, 0, 1, 3)).reshape(HL, 2 * C, H)
    y = jnp.pad(y, ((0, HP - HL), (0, 0), (0, PP - H)))
    w1 = complex_matrix(first_weight[:, 0])
    w2 = complex_matrix(second_weight[:, 0])
    b1 = first_bias.astype(F32).reshape(2 * C, 1)
    b2 = second_bias.astype(F32).reshape(2 * C, 1)
    any_spec = pl.BlockSpec(memory_space=pl.ANY)
    vmem = pl.BlockSpec(memory_space=pltpu.VMEM)
    dma = pltpu.SemaphoreType.DMA
    out, g = pl.pallas_call(
        kernel,
        out_shape=(
            jax.ShapeDtypeStruct((HL, C, W), BF16),
            jax.ShapeDtypeStruct((24, CP), F32),
        ),
        in_specs=[any_spec] * 4 + [vmem] * 6,
        out_specs=(vmem, vmem),
        scratch_shapes=[
            pltpu.VMEM((HP, CP, W), BF16),
            pltpu.VMEM((HP, 2 * C, PP), BF16),
            pltpu.VMEM((CH, ROWS, W), BF16),
            pltpu.VMEM((G * MSG, 2 * PP), BF16),
            pltpu.VMEM((CH, G, MSG, 2 * PP), BF16),
            pltpu.VMEM((CH, G, MSG, 2 * PP), BF16),
            pltpu.VMEM((CH, G, MSG, 2 * PP), BF16),
            pltpu.VMEM((CH, G, MSG, 2 * PP), BF16),
            pltpu.VMEM((HP * ROWS, CP), F32),
            pltpu.VMEM((HL, C, W), F32),
            pltpu.VMEM((4 * C, 2 * PP), BF16),
            pltpu.VMEM((2 * C, 2 * C), F32),
            pltpu.VMEM((2 * C, 2 * C), F32),
            pltpu.VMEM((2 * C, CP), F32),
            pltpu.VMEM((2 * C, CP), F32),
            pltpu.VMEM((G, 24, CP), F32),
            pltpu.VMEM((G, 24, CP), F32),
            pltpu.VMEM((24, CP), F32),
            pltpu.VMEM((G, 24, CP), F32),
            dma((4,)),
            dma((CH, G)),
            dma((CH, G)),
            dma((CH, G)),
            dma((CH, G)),
            dma((G,)),
            dma((G,)),
            dma((G,)),
            dma((G,)),
        ],
        compiler_params=pltpu.CompilerParams(
            collective_id=0, has_side_effects=True, vmem_limit_bytes=60 * 1024 * 1024
        ),
        name="afno_backward",
    )(x, y, jnp.asarray(lon_table()), jnp.asarray(lat_table()), w1.T, w1, w2.T, w2, b1, b2)
    grad_in = jnp.transpose(out, (1, 0, 2))[None]
    parts = g.reshape(4, 6, CP)
    gw = parts[:, :, :C].reshape(2, 2, 1, 6, C)
    gb = parts[:, :, C].reshape(2, 2, 1, 6)
    return (grad_in, gw[0], gb[0], gw[1], gb[1])


def solution(mesh):
    in_specs = (
        P("dp", None, "space", None),
        P("dp", None, None, "space", None),
        P(),
        P(),
        P(),
        P(),
    )
    out_specs = (
        P("dp", None, "space", None),
        P(None, None, "dp", None),
        P(None, None, "dp"),
        P(None, None, "dp", None),
        P(None, None, "dp"),
    )
    return jax.shard_map(
        on_device, mesh=mesh, in_specs=in_specs, out_specs=out_specs, check_vma=False
    )
```

```python
import math

import jax
import jax.numpy as jnp
import ml_dtypes
import numpy as np
from jax import lax
from jax.experimental import pallas as pl
from jax.experimental.pallas import tpu as pltpu
from jax.sharding import PartitionSpec as P

H = 368
W = 768
KW = 368
C = 96
G = 16
HL = 23
HP = 24
CP = 128
KG = 4
ROWS = G * 2 * KG
BASE = (0, 4, 7, 11, 15, 19)
COUNT = (4, 3, 4, 4, 4, 4)
ODD = 1
CHUNKS = ((0,), (1, 2, 3), (4,), (5,))
LANES = (384, 1024, 384, 384)
MOST = 3
MSG = 2 * HP
PP = 384
SCALE = 1.0 / math.sqrt(H * W)
LAM = 0.01
F32 = jnp.float32
BF16 = jnp.bfloat16
MESH = pl.DeviceIdType.MESH


def angles(n, rows, cols):
    index = (rows[:, None].astype(np.int64) * cols[None, :].astype(np.int64)) % n
    theta = index.astype(np.float32) * np.float32(2.0 * math.pi / n)
    return np.cos(theta), np.sin(theta)


def lon_table():
    cos, sin = angles(W, np.arange(KW), np.arange(W))
    both = np.stack([cos, -sin], 1).reshape(G, HL, 2, W).transpose(0, 2, 1, 3)
    full = np.zeros((len(BASE), G, 2, KG, W), np.float32)
    for i, (base, count) in enumerate(zip(BASE, COUNT)):
        full[i, :, :, :count] = both[:, :, base : base + count]
    return full.reshape(len(BASE), ROWS, W).astype(ml_dtypes.bfloat16)


def lat_table():
    cos, sin = angles(H, np.arange(H), np.arange(H))
    full = np.zeros((G, 2, HP, 2, PP), np.float32)
    cos, sin = cos.reshape(G, HL, H), sin.reshape(G, HL, H)
    full[:, 0, :HL, 0, :H] = cos
    full[:, 1, :HL, 0, :H] = sin
    full[:, 0, :HL, 1, :H] = -sin
    full[:, 1, :HL, 1, :H] = cos
    return full.reshape(G * MSG, 2 * PP).astype(ml_dtypes.bfloat16)


def nt(a, b):
    return lax.dot_general(a, b, (((1,), (1,)), ((), ())), preferred_element_type=F32)


def tn(a, b):
    return lax.dot_general(a, b, (((0,), (0,)), ((), ())), preferred_element_type=F32)


def nn(a, b):
    return jnp.dot(a, b, preferred_element_type=F32)


def kernel(
    x_hbm, y_hbm, lon_hbm, lat_hbm, w1_in, b1_in, w2_in, b2_in,
    out_ref, g_ref,
    x_ref, y_ref, lon_ref, lat_ref, fs, fr, bs, br, work, acc, dz_ref, dy_ref, q_ref, rem, pads, few,
    yk_ref, w1t_ref, w1_ref, w2t_ref, w2_ref, b1_ref, b2_ref, gw1, gw2, gb1, gb2, gs, gr, hs, hr,
    load_sem, x_sem, fs_sem, fr_sem, bs_sem, br_sem, gs_sem, gr_sem, hs_sem, hr_sem,
):
    me = lax.axis_index("space")
    row = lax.axis_index("dp")

    barrier = pltpu.get_barrier_semaphore()

    def greet(o, carry):
        pl.semaphore_signal(
            barrier, inc=1, device_id={"space": lax.rem(me + o, G)}, device_id_type=MESH
        )
        pl.semaphore_signal(
            barrier, inc=1, device_id={"dp": lax.rem(row + o, G)}, device_id_type=MESH
        )
        return carry

    lon_first = pltpu.make_async_copy(lon_hbm.at[0], lon_ref.at[0], load_sem.at[0])
    lon_first.start()
    x_loads = []
    for i in range(4):
        part = pl.ds(6 * i, min(6, HL - 6 * i))
        x_loads.append(
            pltpu.make_async_copy(x_hbm.at[part], x_ref.at[part, pl.ds(0, C)], x_sem.at[i])
        )
        x_loads[-1].start()
    lon_rest = pltpu.make_async_copy(
        lon_hbm.at[pl.ds(1, 5)], lon_ref.at[pl.ds(1, 5)], load_sem.at[1]
    )
    lat_load = pltpu.make_async_copy(lat_hbm, lat_ref, load_sem.at[2])
    y_load = pltpu.make_async_copy(y_hbm, y_ref, load_sem.at[3])
    for load in (lon_rest, lat_load, y_load):
        load.start()
    lax.fori_loop(1, G, greet, 0)
    x_ref[:, C:] = jnp.zeros((HP, CP - C, W), BF16)
    x_ref[HL, :C] = jnp.zeros((C, W), BF16)

    lane = lax.broadcasted_iota(jnp.int32, (HP, CP), 1)
    sub = lax.broadcasted_iota(jnp.int32, (HP, CP), 0)
    lane6 = lax.broadcasted_iota(jnp.int32, (6, CP), 1)

    def over_peers(first, body, sign=1):
        def step(o, c):
            body(lax.rem(first + G + sign * o, G))
            return c

        lax.fori_loop(1, G, step, 0)

    def copies(src, dst, send, recv, c):
        def out(peer):
            return pltpu.make_async_remote_copy(
                src_ref=src[c].at[peer], dst_ref=dst[c].at[me], send_sem=send.at[c, peer],
                recv_sem=recv.at[c, me], device_id={"space": peer}, device_id_type=MESH,
            )

        def arrival(peer):
            return pltpu.make_async_remote_copy(
                src_ref=src[c].at[peer], dst_ref=dst[c].at[peer], send_sem=send.at[c, peer],
                recv_sem=recv.at[c, peer], device_id={"space": peer}, device_id_type=MESH,
            )

        return out, arrival

    forward = [copies(fs, fr, fs_sem, fr_sem, c) for c in range(len(CHUNKS))]
    backward = [copies(bs, br, bs_sem, br_sem, c) for c in range(len(CHUNKS))]

    def longitude(groups):
        size = ROWS * len(groups)

        def two(i, carry):
            pair = x_ref[pl.ds(2 * i, 2)].reshape(2 * CP, W)
            table = lon_ref[groups[0] : groups[0] + len(groups)].reshape(size, W)
            got = nt(table, pair)
            work[pl.ds(pl.multiple_of(2 * i * size, ROWS), size), :] = got[:, :CP]
            work[pl.ds(pl.multiple_of((2 * i + 1) * size, ROWS), size), :] = got[:, CP:]
            return carry

        if groups[0] == 0:
            for i in range(4):
                x_loads[i].wait()
                lax.fori_loop(3 * i, 3 * i + 3, two, 0)
        else:
            lax.fori_loop(0, HP // 2, two, 0)

    def quarters(load):
        made = load(0)
        for q in range(1, 4):
            made = jnp.where(lane6 < 32 * q, made, load(q))
        return made

    def padded(tiles, extra, first=0):
        done = []
        for t in range(len(tiles[0])):
            both = []
            for s in range(2):
                v = tiles[s][t]
                if extra is not None and first + t < 6:
                    one = jnp.broadcast_to(extra[s][first + t : first + t + 1], (HP, CP))
                    v = jnp.where(sub == HL, one, v)
                both.append(v)
            done.append(jnp.concatenate(both, 0).astype(BF16))
        return done

    def packed(groups, owner):
        size = ROWS * len(groups)
        tiles, extra = [[], []], None
        for i, group in enumerate(groups):
            for s in range(2):
                at = i * ROWS + owner * 2 * KG + s * KG
                a = [work[pl.ds(at + k, HP, stride=size), :] for k in range(KG)]
                r1 = pltpu.roll(a[1], 96, 1)
                r2 = pltpu.roll(a[2], 64, 1)
                tiles[s].append(jnp.where(lane < 96, a[0], r1))
                tiles[s].append(jnp.where(lane < 64, r1, r2))
                if group == ODD:
                    extra = extra or []
                    extra.append(
                        quarters(
                            lambda q, at=at: pltpu.roll(
                                work[pl.ds(at + 2 + 6 * q * size, 6, stride=size), :],
                                (64 + 32 * q) % CP,
                                1,
                            )
                        )
                    )
                else:
                    tiles[s].append(jnp.where(lane < 32, r2, pltpu.roll(a[3], 32, 1)))
        return padded(tiles, extra)

    for c, groups in enumerate(CHUNKS):
        if c == 0:
            lon_first.wait()
        if c == 1:
            lon_rest.wait()
        longitude(groups)
        if c == 0:
            pl.semaphore_wait(barrier, 2 * (G - 1))

        def send(peer, c=c, groups=groups):
            for t, part in enumerate(packed(groups, peer)):
                fs[c][peer, :, t * CP : (t + 1) * CP] = part
            forward[c][0](peer).start()

        over_peers(me, send)
        for t, part in enumerate(packed(groups, me)):
            fr[c][me, :, t * CP : (t + 1) * CP] = part

    eye = lax.broadcasted_iota(jnp.int32, (C, C), 0) == lax.broadcasted_iota(jnp.int32, (C, C), 1)
    eye = eye.astype(F32).astype(BF16)
    for w, b, m_ref, t_ref, bias_ref in (
        (w1_in, b1_in, w1_ref, w1t_ref, b1_ref),
        (w2_in, b2_in, w2_ref, w2t_ref, b2_ref),
    ):
        wr, wi = w[0].astype(F32), w[1].astype(F32)
        tr, ti = nt(eye, w[0]), nt(eye, w[1])
        m_ref[:C] = jnp.concatenate([wr, wi], 1).astype(BF16)
        m_ref[C:] = jnp.concatenate([-wi, wr], 1).astype(BF16)
        t_ref[:C] = jnp.concatenate([tr, -ti], 1).astype(BF16)
        t_ref[C:] = jnp.concatenate([ti, tr], 1).astype(BF16)
        column = nt(eye, b[...])
        bias_ref[:C] = jnp.broadcast_to(column[:, 0:1], (C, PP))
        bias_ref[C:] = jnp.broadcast_to(column[:, 1:2], (C, PP))
    for ref in (gw1, gw2, gb1, gb2, yk_ref):
        ref[...] = jnp.zeros_like(ref)
    lat_load.wait()
    y_load.wait()

    def folded(v):
        v = v.astype(F32)
        return v[:, :CP] + v[:, CP : 2 * CP] + v[:, 2 * CP :]

    def mix(group):
        def one(k, carry):
            at = BASE[group] + k
            rows = pl.ds(pl.multiple_of(k * C, C), C)
            mult = jnp.where(at + me == 0, SCALE, 2.0 * SCALE).astype(F32)
            dzk = jnp.concatenate([dz_ref[rows, :PP], dz_ref[rows, PP:]], 0) * mult
            yk_ref[:C, :H] = y_ref[0, at]
            yk_ref[C:, :H] = y_ref[1, at]
            yk = yk_ref[...]
            u = nn(w1t_ref[...], yk) + b1_ref[...]
            a = jnp.maximum(u, 0.0).astype(BF16)
            v = nn(w2t_ref[...], a) + b2_ref[...]
            dv = jnp.where(jnp.abs(v) > LAM, dzk, 0.0).astype(BF16)
            gw2[...] += nt(a, dv)
            gb2[...] += folded(dv)
            da = nn(w2_ref[...], dv)
            du = jnp.where(u > 0.0, da, 0.0).astype(BF16)
            gw1[...] += nt(yk, du)
            gb1[...] += folded(du)
            dy = nn(w1_ref[...], du).astype(BF16)
            dy_ref[rows, :PP] = dy[:C]
            dy_ref[rows, PP:] = dy[C:]
            return carry

        lax.fori_loop(0, COUNT[group], one, 0)

    def spread(chunk, g, s, store):
        at = 16 + 16 * s
        v = chunk[g, at : at + 16, : 6 * CP].astype(F32)
        r = HL - 16 if s == 0 else 15
        six = jnp.concatenate([v[r : r + 1, t * CP : (t + 1) * CP] for t in range(6)], 0)
        for q in range(4):
            store(q, six if q == 0 else pltpu.roll(six, CP - 32 * q, 1))

    def middle(c, groups):
        over_peers(me, lambda peer: forward[c][1](peer).wait_recv(), -1)
        if ODD in groups:

            def collect(g, carry):
                for s in range(2):

                    def store(q, v, s=s):
                        rem[pl.ds(g * MSG + s * HP + 6 * q, 6), :] = v

                    spread(fr[c], g, s, store)
                return carry

            lax.fori_loop(0, G, collect, 0)
        lanes = 0
        for group in groups:
            if group == ODD:
                got = fr[c][:, :, : 2 * CP].reshape(G * MSG, 2 * CP)
                got = jnp.concatenate([got, rem[...].astype(BF16)], 1)
            else:
                got = fr[c][:, :, lanes : lanes + PP].reshape(G * MSG, PP)
            dz_ref[...] = tn(got, lat_ref[...])
            mix(group)
            q = nt(lat_ref[...], dy_ref[...])
            width = 2 * CP if group == ODD else PP
            if len(groups) == 1:
                bs[c][...] = q.astype(BF16).reshape(G, MSG, PP)
            else:
                q_ref[...] = q

                def place(g, carry, group=group, lanes=lanes, width=width):
                    tiles, extra = [], []
                    for s in range(2):
                        at = pl.multiple_of(g * MSG + s * HP, 8)
                        v = q_ref[pl.ds(at, HP), :]
                        tiles.append([v[:, t * CP : (t + 1) * CP] for t in range(width // CP)])
                        if group == ODD:

                            def load(q, v=v[:, 2 * CP :]):
                                v = v[6 * q : 6 * q + 6]
                                return v if q == 0 else pltpu.roll(v, 32 * q, 1)

                            pads[g, s, :6] = quarters(load)
                        extra.append(pads[g, s])
                    for t, part in enumerate(padded(tiles, extra, lanes // CP)):
                        bs[c][g, :, lanes + t * CP : lanes + (t + 1) * CP] = part
                    return carry

                lax.fori_loop(0, G, place, 0)
            lanes += width

    def send_back(c):
        over_peers(me, lambda peer: backward[c][0](peer).start())
        br[c][me] = bs[c][me]

    for c in range(3):
        middle(c, CHUNKS[c])
        send_back(c)
    middle(3, CHUNKS[3])

    def combined(g):
        re = g[:C, :C] + g[C:, C:]
        im = g[:C, C:] - g[C:, :C]
        return re, im

    sums = []
    for g, b in ((gw1, gb1), (gw2, gb2)):
        total = jnp.sum(b[...], axis=1, keepdims=True)
        for part, bias in zip(combined(g[...]), (total[:C], total[C:])):
            wide = jnp.concatenate([part, jnp.broadcast_to(bias, (C, CP - C))], 1)
            sums.append(wide)
    for d in range(G):
        gs[d] = jnp.concatenate([s[6 * d : 6 * d + 6] for s in sums], 0)

    def grad_copy(peer, at):
        return pltpu.make_async_remote_copy(
            src_ref=gs.at[peer], dst_ref=gr.at[at], send_sem=gs_sem.at[peer],
            recv_sem=gr_sem.at[at], device_id={"dp": peer}, device_id_type=MESH,
        )

    def share_copy(peer, at):
        return pltpu.make_async_remote_copy(
            src_ref=hs, dst_ref=hr.at[at], send_sem=hs_sem.at[peer],
            recv_sem=hr_sem.at[at], device_id={"space": peer}, device_id_type=MESH,
        )

    over_peers(row, lambda peer: grad_copy(peer, row).start())
    send_back(3)

    def finish(c, groups):
        size = ROWS * len(groups)

        def unpack(g):
            lanes = 0
            for i, group in enumerate(groups):
                width = 2 * CP if group == ODD else PP
                got = br[c][g, :, lanes : lanes + width].astype(F32)
                for s in range(2):
                    p = [
                        got[s * HP : (s + 1) * HP, t * CP : (t + 1) * CP]
                        for t in range(width // CP)
                    ]
                    parts = [
                        p[0],
                        jnp.where(lane < 32, pltpu.roll(p[0], 32, 1), pltpu.roll(p[1], 32, 1)),
                    ]
                    if group == ODD:

                        def store(q, v, s=s):
                            few[s, 6 * q : 6 * q + 6, :] = v

                        spread(br[c], g, s, store)
                        last = few[s]
                    else:
                        last = p[2]
                    parts.append(
                        jnp.where(lane < 64, pltpu.roll(p[1], 64, 1), pltpu.roll(last, 64, 1))
                    )
                    if group == ODD:
                        parts.append(jnp.zeros((HP, CP), F32))
                    else:
                        parts.append(pltpu.roll(last, 96, 1))
                    for k in range(KG):
                        at = i * ROWS + g * 2 * KG + s * KG + k
                        work[pl.ds(at, HP, stride=size), :] = parts[k]
                lanes += width

        unpack(me)

        def step(peer):
            backward[c][1](peer).wait_recv()
            unpack(peer)

        over_peers(me, step, -1)
        table = lon_ref[groups[0] : groups[0] + len(groups)].reshape(size, W)

        def block(first, count):
            columns = []
            for i in range(count):
                v = work[pl.ds(pl.multiple_of((first + i) * size, ROWS), size), :].astype(BF16)
                columns.append(jnp.transpose(v)[:C])
            new = nn(jnp.concatenate(columns, 0), table).reshape(count, C, W) * SCALE
            at = pl.ds(first, count)
            if c == 0:
                acc[at] = x_ref[at, :C].astype(F32) + new
            elif c < len(CHUNKS) - 1:
                acc[at] += new
            else:
                out_ref[at] = (acc[at] + new).astype(BF16)

        def four(i, carry):
            block(4 * i, 4)
            return carry

        lax.fori_loop(0, HL // 4, four, 0)
        block(HL // 4 * 4, HL % 4)

    for c in range(3):
        finish(c, CHUNKS[c])
    over_peers(row, lambda peer: grad_copy(peer, peer).wait_recv(), -1)
    gr[row] = gs[row]
    hs[...] = jnp.sum(gr[...], axis=0)
    over_peers(me, lambda peer: share_copy(peer, me).start())
    finish(3, CHUNKS[3])
    over_peers(me, lambda peer: share_copy(peer, peer).wait_recv(), -1)
    hr[me] = hs[...]
    total = jnp.sum(hr[...], axis=0)
    for i in range(4):
        g_ref[i] = total[6 * i : 6 * i + 6]

    for c in range(len(CHUNKS)):
        over_peers(me, lambda peer, c=c: forward[c][0](peer).wait_send())
        over_peers(me, lambda peer, c=c: backward[c][0](peer).wait_send())
    over_peers(row, lambda peer: grad_copy(peer, row).wait_send())
    over_peers(me, lambda peer: share_copy(peer, me).wait_send())


def on_device(cotangent, spectrum, first_weight, first_bias, second_weight, second_bias):
    x = jnp.transpose(cotangent[0], (1, 0, 2))
    y = jnp.transpose(spectrum[0], (0, 2, 1, 3))
    any_spec = pl.BlockSpec(memory_space=pl.ANY)
    vmem = pl.BlockSpec(memory_space=pltpu.VMEM)
    dma = pltpu.SemaphoreType.DMA
    messages = [pltpu.VMEM((G, MSG, lanes), BF16) for lanes in LANES]
    n = len(CHUNKS)
    out, g = pl.pallas_call(
        kernel,
        out_shape=(
            pltpu.VMEM((HL, C, W), BF16),
            jax.ShapeDtypeStruct((4, 6, CP), F32),
        ),
        in_specs=[any_spec] * 4 + [vmem] * 4,
        out_specs=(vmem, vmem),
        scratch_shapes=[
            pltpu.VMEM((HP, CP, W), BF16),
            pltpu.VMEM((2, HL, C, H), BF16),
            pltpu.VMEM((len(BASE), ROWS, W), BF16),
            pltpu.VMEM((G * MSG, 2 * PP), BF16),
            messages,
            messages,
            messages,
            messages,
            pltpu.VMEM((HP * MOST * ROWS, CP), F32),
            pltpu.VMEM((HL, C, W), F32),
            pltpu.VMEM((KG * C, 2 * PP), F32),
            pltpu.VMEM((KG * C, 2 * PP), BF16),
            pltpu.VMEM((G * MSG, PP), F32),
            pltpu.VMEM((G * MSG, CP), F32),
            pltpu.VMEM((G, 2, 8, CP), F32),
            pltpu.VMEM((2, HP, CP), F32),
            pltpu.VMEM((2 * C, PP), BF16),
            pltpu.VMEM((2 * C, 2 * C), BF16),
            pltpu.VMEM((2 * C, 2 * C), BF16),
            pltpu.VMEM((2 * C, 2 * C), BF16),
            pltpu.VMEM((2 * C, 2 * C), BF16),
            pltpu.VMEM((2 * C, PP), F32),
            pltpu.VMEM((2 * C, PP), F32),
            pltpu.VMEM((2 * C, 2 * C), F32),
            pltpu.VMEM((2 * C, 2 * C), F32),
            pltpu.VMEM((2 * C, CP), F32),
            pltpu.VMEM((2 * C, CP), F32),
            pltpu.VMEM((G, 24, CP), F32),
            pltpu.VMEM((G, 24, CP), F32),
            pltpu.VMEM((24, CP), F32),
            pltpu.VMEM((G, 24, CP), F32),
            dma((4,)),
            dma((4,)),
            dma((n, G)),
            dma((n, G)),
            dma((n, G)),
            dma((n, G)),
            dma((G,)),
            dma((G,)),
            dma((G,)),
            dma((G,)),
        ],
        compiler_params=pltpu.CompilerParams(
            collective_id=0, has_side_effects=True, vmem_limit_bytes=52 * 1024 * 1024
        ),
        name="afno_backward",
    )(
        x, y, jnp.asarray(lon_table()), jnp.asarray(lat_table()),
        first_weight[:, 0], first_bias[:, 0], second_weight[:, 0], second_bias[:, 0],
    )
    grad_in = jnp.transpose(out, (1, 0, 2))[None]
    gw = g[:, :, :C].reshape(2, 2, 1, 6, C)
    gb = g[:, :, C].reshape(2, 2, 1, 6)
    return (grad_in, gw[0], gb[0], gw[1], gb[1])


def solution(mesh):
    in_specs = (
        P("dp", None, "space", None),
        P("dp", None, None, "space", None),
        P(),
        P(),
        P(),
        P(),
    )
    out_specs = (
        P("dp", None, "space", None),
        P(None, None, "dp", None),
        P(None, None, "dp"),
        P(None, None, "dp", None),
        P(None, None, "dp"),
    )
    return jax.shard_map(
        on_device, mesh=mesh, in_specs=in_specs, out_specs=out_specs, check_vma=False
    )
```

```python
import math

import jax
import jax.numpy as jnp
import ml_dtypes
import numpy as np
from jax import lax
from jax.experimental import pallas as pl
from jax.experimental.pallas import tpu as pltpu
from jax.sharding import PartitionSpec as P

H = 368
W = 768
KW = 368
C = 96
G = 16
HL = 23
HP = 24
CP = 128
KG = 4
ROWS = G * 2 * KG
BASE = (0, 4, 7, 11, 15, 19)
COUNT = (4, 3, 4, 4, 4, 4)
ODD = 1
CHUNKS = ((0,), (1, 2, 3), (4,), (5,))
LANES = (384, 1024, 384, 384)
MOST = 3
MSG = 2 * HP
PP = 384
SCALE = 1.0 / math.sqrt(H * W)
LAM = 0.01
F32 = jnp.float32
BF16 = jnp.bfloat16
MESH = pl.DeviceIdType.MESH


def angles(n, rows, cols):
    index = (rows[:, None].astype(np.int64) * cols[None, :].astype(np.int64)) % n
    theta = index.astype(np.float32) * np.float32(2.0 * math.pi / n)
    return np.cos(theta), np.sin(theta)


def lon_table():
    cos, sin = angles(W, np.arange(KW), np.arange(W))
    both = np.stack([cos, -sin], 1).reshape(G, HL, 2, W).transpose(0, 2, 1, 3)
    full = np.zeros((len(BASE), G, 2, KG, W), np.float32)
    for i, (base, count) in enumerate(zip(BASE, COUNT)):
        full[i, :, :, :count] = both[:, :, base : base + count]
    return full.reshape(len(BASE), ROWS, W).astype(ml_dtypes.bfloat16)


def lat_table():
    cos, sin = angles(H, np.arange(H), np.arange(H))
    full = np.zeros((G, 2, HP, 2, PP), np.float32)
    cos, sin = cos.reshape(G, HL, H), sin.reshape(G, HL, H)
    full[:, 0, :HL, 0, :H] = cos
    full[:, 1, :HL, 0, :H] = sin
    full[:, 0, :HL, 1, :H] = -sin
    full[:, 1, :HL, 1, :H] = cos
    return full.reshape(G * MSG, 2 * PP).astype(ml_dtypes.bfloat16)


def nt(a, b):
    return lax.dot_general(a, b, (((1,), (1,)), ((), ())), preferred_element_type=F32)


def tn(a, b):
    return lax.dot_general(a, b, (((0,), (0,)), ((), ())), preferred_element_type=F32)


def nn(a, b):
    return jnp.dot(a, b, preferred_element_type=F32)


def kernel(
    x_hbm, y_hbm, lon_hbm, lat_hbm, w1_hbm, b1_hbm, w2_hbm, b2_hbm,
    out_ref, g_ref,
    w1_in, b1_in, w2_in, b2_in, x_ref, y_ref, lon_ref, lat_ref, fs, fr, bs, br, work, acc, dz_ref, dy_ref, q_ref, rem, pads, few,
    yk_ref, w1t_ref, w1_ref, w2t_ref, w2_ref, b1_ref, b2_ref, gw1, gw2, gb1, gb2,
    gs, gr, hs, hr, zs, zr, ts, tr,
    load_sem, small_sem, x_sem, fs_sem, fr_sem, bs_sem, br_sem,
    gs_sem, gr_sem, hs_sem, hr_sem, zs_sem, zr_sem, ts_sem, tr_sem,
):
    me = lax.axis_index("space")
    row = lax.axis_index("dp")

    my_x, my_zh = me // 4, lax.rem(me, 4)
    my_zl, my_yc = row // 8, lax.rem(row, 8)

    def yc_peer(yc):
        return {"dp": my_zl * 8 + yc}

    def x_peer(x):
        return {"space": x * 4 + my_zh}

    def z_peer(z):
        return {"dp": (z // 4) * 8 + my_yc, "space": my_x * 4 + lax.rem(z, 4)}

    my_z = my_zl * 4 + my_zh
    barrier = pltpu.get_barrier_semaphore()

    def greet(device):
        pl.semaphore_signal(barrier, inc=1, device_id=device, device_id_type=MESH)

    def greet_space(o, carry):
        greet({"space": lax.rem(me + o, G)})
        return carry

    def greet_yc(o, carry):
        greet(yc_peer(lax.rem(my_yc + o, 8)))
        return carry

    def greet_z(o, carry):
        greet(z_peer((1 - my_zl) * 4 + o))
        return carry

    lon_first = pltpu.make_async_copy(lon_hbm.at[0], lon_ref.at[0], load_sem.at[0])
    lon_first.start()
    x_loads = []
    for i in range(4):
        part = pl.ds(6 * i, min(6, HL - 6 * i))
        x_loads.append(
            pltpu.make_async_copy(x_hbm.at[part], x_ref.at[part, pl.ds(0, C)], x_sem.at[i])
        )
        x_loads[-1].start()
    lon_rest = pltpu.make_async_copy(
        lon_hbm.at[pl.ds(1, 5)], lon_ref.at[pl.ds(1, 5)], load_sem.at[1]
    )
    lat_load = pltpu.make_async_copy(lat_hbm, lat_ref, load_sem.at[2])
    y_load = pltpu.make_async_copy(y_hbm, y_ref, load_sem.at[3])
    small = [
        pltpu.make_async_copy(src, dst, small_sem.at[i])
        for i, (src, dst) in enumerate(
            [(w1_hbm, w1_in), (b1_hbm, b1_in), (w2_hbm, w2_in), (b2_hbm, b2_in)]
        )
    ]
    lax.fori_loop(1, G, greet_space, 0)
    lax.fori_loop(1, 8, greet_yc, 0)
    lax.fori_loop(0, 4, greet_z, 0)
    x_ref[:, C:] = jnp.zeros((HP, CP - C, W), BF16)
    x_ref[HL, :C] = jnp.zeros((C, W), BF16)

    lane = lax.broadcasted_iota(jnp.int32, (HP, CP), 1)
    sub = lax.broadcasted_iota(jnp.int32, (HP, CP), 0)
    lane6 = lax.broadcasted_iota(jnp.int32, (6, CP), 1)

    def over_peers(first, body, sign=1, n=G):
        def step(o, c):
            body(lax.rem(first + n + sign * o, n))
            return c

        lax.fori_loop(1, n, step, 0)

    def copies(src, dst, send, recv, c):
        def out(peer):
            return pltpu.make_async_remote_copy(
                src_ref=src[c].at[peer], dst_ref=dst[c].at[me], send_sem=send.at[c, peer],
                recv_sem=recv.at[c, me], device_id={"space": peer}, device_id_type=MESH,
            )

        def arrival(peer):
            return pltpu.make_async_remote_copy(
                src_ref=src[c].at[peer], dst_ref=dst[c].at[peer], send_sem=send.at[c, peer],
                recv_sem=recv.at[c, peer], device_id={"space": peer}, device_id_type=MESH,
            )

        return out, arrival

    forward = [copies(fs, fr, fs_sem, fr_sem, c) for c in range(len(CHUNKS))]
    backward = [copies(bs, br, bs_sem, br_sem, c) for c in range(len(CHUNKS))]

    def longitude(groups):
        size = ROWS * len(groups)

        def two(i, carry):
            pair = x_ref[pl.ds(2 * i, 2)].reshape(2 * CP, W)
            table = lon_ref[groups[0] : groups[0] + len(groups)].reshape(size, W)
            got = nt(table, pair)
            work[pl.ds(pl.multiple_of(2 * i * size, ROWS), size), :] = got[:, :CP]
            work[pl.ds(pl.multiple_of((2 * i + 1) * size, ROWS), size), :] = got[:, CP:]
            return carry

        if groups[0] == 0:
            for i in range(4):
                x_loads[i].wait()
                if i == 3:
                    for load in (lon_rest, lat_load, y_load, *small):
                        load.start()
                lax.fori_loop(3 * i, 3 * i + 3, two, 0)
        else:
            lax.fori_loop(0, HP // 2, two, 0)

    def quarters(load):
        made = load(0)
        for q in range(1, 4):
            made = jnp.where(lane6 < 32 * q, made, load(q))
        return made

    def padded(tiles, extra, first=0):
        done = []
        for t in range(len(tiles[0])):
            both = []
            for s in range(2):
                v = tiles[s][t]
                if extra is not None and first + t < 6:
                    one = jnp.broadcast_to(extra[s][first + t : first + t + 1], (HP, CP))
                    v = jnp.where(sub == HL, one, v)
                both.append(v)
            done.append(jnp.concatenate(both, 0).astype(BF16))
        return done

    def packed(groups, owner):
        size = ROWS * len(groups)
        tiles, extra = [[], []], None
        for i, group in enumerate(groups):
            for s in range(2):
                at = i * ROWS + owner * 2 * KG + s * KG
                a = [work[pl.ds(at + k, HP, stride=size), :] for k in range(KG)]
                r1 = pltpu.roll(a[1], 96, 1)
                r2 = pltpu.roll(a[2], 64, 1)
                tiles[s].append(jnp.where(lane < 96, a[0], r1))
                tiles[s].append(jnp.where(lane < 64, r1, r2))
                if group == ODD:
                    extra = extra or []
                    extra.append(
                        quarters(
                            lambda q, at=at: pltpu.roll(
                                work[pl.ds(at + 2 + 6 * q * size, 6, stride=size), :],
                                (64 + 32 * q) % CP,
                                1,
                            )
                        )
                    )
                else:
                    tiles[s].append(jnp.where(lane < 32, r2, pltpu.roll(a[3], 32, 1)))
        return padded(tiles, extra)

    for c, groups in enumerate(CHUNKS):
        if c == 0:
            lon_first.wait()
        if c == 1:
            lon_rest.wait()
        longitude(groups)
        if c == 0:
            pl.semaphore_wait(barrier, 15 + 7 + 4)

        def send(peers, c=c, groups=groups):
            for peer in peers:
                for t, part in enumerate(packed(groups, peer)):
                    fs[c][peer, :, t * CP : (t + 1) * CP] = part
            for peer in peers:
                forward[c][0](peer).start()

        def send_two(i, carry, send=send):
            send([lax.rem(me + 2 * i, G), lax.rem(me + 2 * i + 1, G)])
            return carry

        send([lax.rem(me + 1, G)])
        lax.fori_loop(1, G // 2, send_two, 0)
        for t, part in enumerate(packed(groups, me)):
            fr[c][me, :, t * CP : (t + 1) * CP] = part

    for load in (lat_load, y_load, *small):
        load.wait()
    eye = lax.broadcasted_iota(jnp.int32, (C, C), 0) == lax.broadcasted_iota(jnp.int32, (C, C), 1)
    eye = eye.astype(F32).astype(BF16)
    for w, b, m_ref, t_ref, bias_ref in (
        (w1_in, b1_in, w1_ref, w1t_ref, b1_ref),
        (w2_in, b2_in, w2_ref, w2t_ref, b2_ref),
    ):
        wr, wi = w[0].astype(F32), w[1].astype(F32)
        wrt, wit = nt(eye, w[0]), nt(eye, w[1])
        m_ref[:C] = jnp.concatenate([wr, wi], 1).astype(BF16)
        m_ref[C:] = jnp.concatenate([-wi, wr], 1).astype(BF16)
        t_ref[:C] = jnp.concatenate([wrt, -wit], 1).astype(BF16)
        t_ref[C:] = jnp.concatenate([wit, wrt], 1).astype(BF16)
        column = nt(eye, b[...])
        bias_ref[:C] = jnp.broadcast_to(column[:, 0:1], (C, PP))
        bias_ref[C:] = jnp.broadcast_to(column[:, 1:2], (C, PP))
    for ref in (gw1, gw2, gb1, gb2, yk_ref):
        ref[...] = jnp.zeros_like(ref)

    def folded(v):
        v = v.astype(F32)
        return v[:, :CP] + v[:, CP : 2 * CP] + v[:, 2 * CP :]

    def mix(group):
        for k in range(COUNT[group]):
            at = BASE[group] + k
            rows = slice(k * C, (k + 1) * C)
            mult = jnp.where(at + me == 0, SCALE, 2.0 * SCALE).astype(F32)
            dzk = jnp.concatenate([dz_ref[rows, :PP], dz_ref[rows, PP:]], 0) * mult
            yk_ref[k, :C, :H] = y_ref[0, at]
            yk_ref[k, C:, :H] = y_ref[1, at]
            yk = yk_ref[k]
            u = nn(w1t_ref[...], yk) + b1_ref[...]
            a = jnp.maximum(u, 0.0).astype(BF16)
            v = nn(w2t_ref[...], a) + b2_ref[...]
            dv = jnp.where(jnp.abs(v) > LAM, dzk, 0.0).astype(BF16)
            gw2[...] += nt(a, dv)
            gb2[...] += folded(dv)
            da = nn(w2_ref[...], dv)
            du = jnp.where(u > 0.0, da, 0.0).astype(BF16)
            gw1[...] += nt(yk, du)
            gb1[...] += folded(du)
            dy = nn(w1_ref[...], du).astype(BF16)
            dy_ref[rows, :PP] = dy[:C]
            dy_ref[rows, PP:] = dy[C:]

    def spread(chunk, g, s, store):
        at = 16 + 16 * s
        v = chunk[g, at : at + 16, : 6 * CP].astype(F32)
        r = HL - 16 if s == 0 else 15
        six = jnp.concatenate([v[r : r + 1, t * CP : (t + 1) * CP] for t in range(6)], 0)
        for q in range(4):
            store(q, six if q == 0 else pltpu.roll(six, CP - 32 * q, 1))

    def middle(c, groups):
        over_peers(me, lambda peer: forward[c][1](peer).wait_recv(), -1)
        if ODD in groups:

            def collect(g, carry):
                for s in range(2):

                    def store(q, v, s=s):
                        rem[pl.ds(g * MSG + s * HP + 6 * q, 6), :] = v

                    spread(fr[c], g, s, store)
                return carry

            lax.fori_loop(0, G, collect, 0)
        lanes = 0
        for group in groups:
            if group == ODD:
                got = fr[c][:, :, : 2 * CP].reshape(G * MSG, 2 * CP)
                got = jnp.concatenate([got, rem[...].astype(BF16)], 1)
            else:
                got = fr[c][:, :, lanes : lanes + PP].reshape(G * MSG, PP)
            dz_ref[...] = tn(got, lat_ref[...])
            mix(group)
            q = nt(lat_ref[...], dy_ref[...])
            width = 2 * CP if group == ODD else PP
            if len(groups) == 1:
                bs[c][...] = q.astype(BF16).reshape(G, MSG, PP)
            else:
                q_ref[...] = q

                def place(g, carry, group=group, lanes=lanes, width=width):
                    tiles, extra = [], []
                    for s in range(2):
                        at = pl.multiple_of(g * MSG + s * HP, 8)
                        v = q_ref[pl.ds(at, HP), :]
                        tiles.append([v[:, t * CP : (t + 1) * CP] for t in range(width // CP)])
                        if group == ODD:

                            def load(q, v=v[:, 2 * CP :]):
                                v = v[6 * q : 6 * q + 6]
                                return v if q == 0 else pltpu.roll(v, 32 * q, 1)

                            pads[g, s, :6] = quarters(load)
                        extra.append(pads[g, s])
                    for t, part in enumerate(padded(tiles, extra, lanes // CP)):
                        bs[c][g, :, lanes + t * CP : lanes + (t + 1) * CP] = part
                    return carry

                lax.fori_loop(0, G, place, 0)
            lanes += width

    def send_back(c):
        over_peers(me, lambda peer: backward[c][0](peer).start())
        br[c][me] = bs[c][me]

    for c in range(3):
        middle(c, CHUNKS[c])
        send_back(c)
    middle(3, CHUNKS[3])

    def combined(g):
        re = g[:C, :C] + g[C:, C:]
        im = g[:C, C:] - g[C:, :C]
        return re, im

    sums = []
    for g, b in ((gw1, gb1), (gw2, gb2)):
        total = jnp.sum(b[...], axis=1, keepdims=True)
        for part, bias in zip(combined(g[...]), (total[:C], total[C:])):
            wide = jnp.concatenate([part, jnp.broadcast_to(bias, (C, CP - C))], 1)
            sums.append(wide)
    zero2 = jnp.zeros((2, CP), F32)
    for d in range(G):
        for i, v in enumerate(sums):
            gs[d % 8, d // 8, 8 * i : 8 * i + 8] = jnp.concatenate([v[6 * d : 6 * d + 6], zero2], 0)

    def yc_copy(peer, at):
        return pltpu.make_async_remote_copy(
            src_ref=gs.at[peer], dst_ref=gr.at[at], send_sem=gs_sem.at[peer],
            recv_sem=gr_sem.at[at], device_id=yc_peer(peer), device_id_type=MESH,
        )

    def x_copy(peer, at):
        return pltpu.make_async_remote_copy(
            src_ref=hs.at[peer], dst_ref=hr.at[at], send_sem=hs_sem.at[peer],
            recv_sem=hr_sem.at[at], device_id=x_peer(peer), device_id_type=MESH,
        )

    def z_copy(peer, at):
        return pltpu.make_async_remote_copy(
            src_ref=zs.at[peer // 4], dst_ref=zr.at[at], send_sem=zs_sem.at[peer],
            recv_sem=zr_sem.at[at], device_id=z_peer(peer), device_id_type=MESH,
        )

    def share_copy(peer, at):
        return pltpu.make_async_remote_copy(
            src_ref=ts, dst_ref=tr.at[at], send_sem=ts_sem.at[peer],
            recv_sem=tr_sem.at[at], device_id=x_peer(peer), device_id_type=MESH,
        )

    over_peers(my_yc, lambda peer: yc_copy(peer, my_yc).start(), 1, 8)
    gr[my_yc] = gs[my_yc]
    over_peers(my_yc, lambda peer: yc_copy(peer, peer).wait_recv(), -1, 8)
    total = jnp.sum(gr[...], axis=0)
    for x in range(4):
        hs[x] = total[:, 8 * x : 8 * x + 8]
    over_peers(my_x, lambda peer: x_copy(peer, my_x).start(), 1, 4)
    hr[my_x] = hs[my_x]
    over_peers(my_x, lambda peer: x_copy(peer, peer).wait_recv(), -1, 4)
    zs[...] = jnp.sum(hr[...], axis=0)
    over_peers(my_z, lambda peer: z_copy(peer, my_z).start(), 1, 8)
    zr[my_z] = zs[my_zl]
    send_back(3)

    def finish(c, groups):
        size = ROWS * len(groups)

        def unpack(g):
            lanes = 0
            for i, group in enumerate(groups):
                width = 2 * CP if group == ODD else PP
                got = br[c][g, :, lanes : lanes + width].astype(F32)
                for s in range(2):
                    p = [
                        got[s * HP : (s + 1) * HP, t * CP : (t + 1) * CP]
                        for t in range(width // CP)
                    ]
                    parts = [
                        p[0],
                        jnp.where(lane < 32, pltpu.roll(p[0], 32, 1), pltpu.roll(p[1], 32, 1)),
                    ]
                    if group == ODD:

                        def store(q, v, s=s):
                            few[s, 6 * q : 6 * q + 6, :] = v

                        spread(br[c], g, s, store)
                        last = few[s]
                    else:
                        last = p[2]
                    parts.append(
                        jnp.where(lane < 64, pltpu.roll(p[1], 64, 1), pltpu.roll(last, 64, 1))
                    )
                    if group == ODD:
                        parts.append(jnp.zeros((HP, CP), F32))
                    else:
                        parts.append(pltpu.roll(last, 96, 1))
                    for k in range(KG):
                        at = i * ROWS + g * 2 * KG + s * KG + k
                        work[pl.ds(at, HP, stride=size), :] = parts[k]
                lanes += width

        def arrived(peers):
            for peer in peers:
                backward[c][1](peer).wait_recv()

        def two(i, carry):
            peers = [lax.rem(me + G - 2 * i, G), lax.rem(me + G - 2 * i - 1, G)]
            arrived(peers)
            for peer in peers:
                unpack(peer)
            return carry

        first = lax.rem(me + G - 1, G)
        arrived([first])
        unpack(me)
        unpack(first)
        lax.fori_loop(1, G // 2, two, 0)
        table = lon_ref[groups[0] : groups[0] + len(groups)].reshape(size, W)

        def block(first, count):
            columns = []
            for i in range(count):
                v = work[pl.ds(pl.multiple_of((first + i) * size, ROWS), size), :].astype(BF16)
                columns.append(jnp.transpose(v)[:C])
            new = nn(jnp.concatenate(columns, 0), table).reshape(count, C, W) * SCALE
            at = pl.ds(first, count)
            if c == 0:
                acc[at] = x_ref[at, :C].astype(F32) + new
            elif c < len(CHUNKS) - 1:
                acc[at] += new
            else:
                out_ref[at] = (acc[at] + new).astype(BF16)

        def four(i, carry):
            block(4 * i, 4)
            return carry

        lax.fori_loop(0, HL // 4, four, 0)
        block(HL // 4 * 4, HL % 4)

    for c in range(len(CHUNKS)):
        over_peers(me, lambda peer, c=c: forward[c][0](peer).wait_send())
    over_peers(my_yc, lambda peer: yc_copy(peer, my_yc).wait_send(), 1, 8)
    over_peers(my_x, lambda peer: x_copy(peer, my_x).wait_send(), 1, 4)
    for c in range(3):
        finish(c, CHUNKS[c])
        over_peers(me, lambda peer, c=c: backward[c][0](peer).wait_send())
    over_peers(my_z, lambda peer: z_copy(peer, my_z).wait_send(), 1, 8)
    over_peers(my_z, lambda peer: z_copy(peer, peer).wait_recv(), -1, 8)
    ts[...] = jnp.sum(zr[...], axis=0)
    over_peers(my_x, lambda peer: share_copy(peer, my_x).start(), 1, 4)
    tr[my_x] = ts[...]
    finish(3, CHUNKS[3])
    over_peers(my_x, lambda peer: share_copy(peer, peer).wait_recv(), -1, 4)
    g_ref[...] = tr[...]
    over_peers(me, lambda peer: backward[3][0](peer).wait_send())
    over_peers(my_x, lambda peer: share_copy(peer, my_x).wait_send(), 1, 4)


def emit(g_in, gw1_ref, gb1_ref, gw2_ref, gb2_ref):
    rows = lax.broadcasted_iota(jnp.int32, (8, CP), 0)
    lanes = lax.broadcasted_iota(jnp.int32, (8, CP), 1)
    for i, (w_ref, b_ref) in enumerate(((gw1_ref, gb1_ref), (gw2_ref, gb2_ref))):
        for s in range(2):
            v = g_in[2 * i + s]
            for r in range(6):
                w_ref[s, r, :, :] = v[r : r + 1, :C]
            spread = jnp.where(rows == lanes, jnp.broadcast_to(v[:, C : C + 1], (8, CP)), 0.0)
            b_ref[s, :, :] = jnp.sum(spread, axis=0, keepdims=True)[:, :6]


def on_device(cotangent, spectrum, first_weight, first_bias, second_weight, second_bias):
    x = jnp.transpose(cotangent[0], (1, 0, 2))
    y = jnp.transpose(spectrum[0], (0, 2, 1, 3))
    any_spec = pl.BlockSpec(memory_space=pl.ANY)
    vmem = pl.BlockSpec(memory_space=pltpu.VMEM)
    dma = pltpu.SemaphoreType.DMA
    messages = [pltpu.VMEM((G, MSG, lanes), BF16) for lanes in LANES]
    n = len(CHUNKS)
    out, g = pl.pallas_call(
        kernel,
        out_shape=(
            pltpu.VMEM((HL, C, W), BF16),
            pltpu.VMEM((4, 8, CP), F32),
        ),
        in_specs=[any_spec] * 8,
        out_specs=(vmem, vmem),
        scratch_shapes=[
            pltpu.VMEM((2, C, C), BF16),
            pltpu.VMEM((2, C), BF16),
            pltpu.VMEM((2, C, C), BF16),
            pltpu.VMEM((2, C), BF16),
            pltpu.VMEM((HP, CP, W), BF16),
            pltpu.VMEM((2, HL, C, H), BF16),
            pltpu.VMEM((len(BASE), ROWS, W), BF16),
            pltpu.VMEM((G * MSG, 2 * PP), BF16),
            messages,
            messages,
            messages,
            messages,
            pltpu.VMEM((HP * MOST * ROWS, CP), F32),
            pltpu.VMEM((HL, C, W), F32),
            pltpu.VMEM((KG * C, 2 * PP), F32),
            pltpu.VMEM((KG * C, 2 * PP), BF16),
            pltpu.VMEM((G * MSG, PP), F32),
            pltpu.VMEM((G * MSG, CP), F32),
            pltpu.VMEM((G, 2, 8, CP), F32),
            pltpu.VMEM((2, HP, CP), F32),
            pltpu.VMEM((KG, 2 * C, PP), BF16),
            pltpu.VMEM((2 * C, 2 * C), BF16),
            pltpu.VMEM((2 * C, 2 * C), BF16),
            pltpu.VMEM((2 * C, 2 * C), BF16),
            pltpu.VMEM((2 * C, 2 * C), BF16),
            pltpu.VMEM((2 * C, PP), F32),
            pltpu.VMEM((2 * C, PP), F32),
            pltpu.VMEM((2 * C, 2 * C), F32),
            pltpu.VMEM((2 * C, 2 * C), F32),
            pltpu.VMEM((2 * C, CP), F32),
            pltpu.VMEM((2 * C, CP), F32),
            pltpu.VMEM((8, 2, 32, CP), F32),
            pltpu.VMEM((8, 2, 32, CP), F32),
            pltpu.VMEM((4, 2, 8, CP), F32),
            pltpu.VMEM((4, 2, 8, CP), F32),
            pltpu.VMEM((2, 8, CP), F32),
            pltpu.VMEM((8, 8, CP), F32),
            pltpu.VMEM((8, CP), F32),
            pltpu.VMEM((4, 8, CP), F32),
            dma((4,)),
            dma((4,)),
            dma((4,)),
            dma((n, G)),
            dma((n, G)),
            dma((n, G)),
            dma((n, G)),
            dma((8,)),
            dma((8,)),
            dma((4,)),
            dma((4,)),
            dma((8,)),
            dma((8,)),
            dma((4,)),
            dma((4,)),
        ],
        compiler_params=pltpu.CompilerParams(
            collective_id=0, has_side_effects=True, vmem_limit_bytes=52 * 1024 * 1024
        ),
        name="afno_backward",
    )(
        x, y, jnp.asarray(lon_table()), jnp.asarray(lat_table()),
        first_weight[:, 0], first_bias[:, 0], second_weight[:, 0], second_bias[:, 0],
    )
    gw1, gb1, gw2, gb2 = pl.pallas_call(
        emit,
        out_shape=(
            jax.ShapeDtypeStruct((2, 6, 1, C), F32),
            jax.ShapeDtypeStruct((2, 1, 6), F32),
            jax.ShapeDtypeStruct((2, 6, 1, C), F32),
            jax.ShapeDtypeStruct((2, 1, 6), F32),
        ),
        in_specs=[vmem],
        out_specs=(vmem, vmem, vmem, vmem),
        name="emit",
    )(pltpu.with_memory_space_constraint(g, pltpu.VMEM))
    grad_in = jnp.transpose(out, (1, 0, 2))[None]
    gw1, gw2 = [jnp.transpose(v, (0, 2, 1, 3)) for v in (gw1, gw2)]
    return (grad_in, gw1, gb1, gw2, gb2)


def solution(mesh):
    in_specs = (
        P("dp", None, "space", None),
        P("dp", None, None, "space", None),
        P(),
        P(),
        P(),
        P(),
    )
    out_specs = (
        P("dp", None, "space", None),
        P(None, None, "dp", None),
        P(None, None, "dp"),
        P(None, None, "dp", None),
        P(None, None, "dp"),
    )
    return jax.shard_map(
        on_device, mesh=mesh, in_specs=in_specs, out_specs=out_specs, check_vma=False
    )
```

```python
import math

import jax
import jax.numpy as jnp
import ml_dtypes
import numpy as np
from jax import lax
from jax.experimental import pallas as pl
from jax.experimental.pallas import tpu as pltpu
from jax.sharding import PartitionSpec as P

H = 368
W = 768
KW = 368
C = 96
G = 16
HL = 23
HP = 24
CP = 128
KG = 4
ROWS = G * 2 * KG
BASE = (0, 4, 7, 11, 15, 19)
COUNT = (4, 3, 4, 4, 4, 4)
ODD = 1
CHUNKS = ((0,), (1, 2, 3), (4,), (5,))
LANES = (384, 1024, 384, 384)
MOST = 3
MSG = 2 * HP
PP = 384
SCALE = 1.0 / math.sqrt(H * W)
LAM = 0.01
F32 = jnp.float32
BF16 = jnp.bfloat16
MESH = pl.DeviceIdType.MESH


def angles(n, rows, cols):
    index = (rows[:, None].astype(np.int64) * cols[None, :].astype(np.int64)) % n
    theta = index.astype(np.float32) * np.float32(2.0 * math.pi / n)
    return np.cos(theta), np.sin(theta)


def lon_table():
    cos, sin = angles(W, np.arange(KW), np.arange(W))
    both = np.stack([cos, -sin], 1).reshape(G, HL, 2, W).transpose(0, 2, 1, 3)
    full = np.zeros((len(BASE), G, 2, KG, W), np.float32)
    for i, (base, count) in enumerate(zip(BASE, COUNT)):
        full[i, :, :, :count] = both[:, :, base : base + count]
    return full.reshape(len(BASE), ROWS, W).astype(ml_dtypes.bfloat16)


def lat_table():
    cos, sin = angles(H, np.arange(H), np.arange(H))
    full = np.zeros((G, 2, HP, 2, PP), np.float32)
    cos, sin = cos.reshape(G, HL, H), sin.reshape(G, HL, H)
    full[:, 0, :HL, 0, :H] = cos
    full[:, 1, :HL, 0, :H] = sin
    full[:, 0, :HL, 1, :H] = -sin
    full[:, 1, :HL, 1, :H] = cos
    return full.reshape(G * MSG, 2 * PP).astype(ml_dtypes.bfloat16)


def nt(a, b):
    return lax.dot_general(a, b, (((1,), (1,)), ((), ())), preferred_element_type=F32)


def tn(a, b):
    return lax.dot_general(a, b, (((0,), (0,)), ((), ())), preferred_element_type=F32)


def nn(a, b):
    return jnp.dot(a, b, preferred_element_type=F32)


def kernel(
    x_hbm, y_hbm, lon_hbm, lat_hbm, w1_hbm, b1_hbm, w2_hbm, b2_hbm,
    out_ref, g_ref,
    w1_in, b1_in, w2_in, b2_in, x_ref, y_ref, lon_ref, lat_ref, fs, fr, bs, br, work, acc, dz_ref, dy_ref, q_ref, rem, pads, few,
    yk_ref, w1t_ref, w1_ref, w2t_ref, w2_ref, b1_ref, b2_ref, gw1, gw2, gb1, gb2,
    gs, gr, hs, hr, zs, zr, ts, tr,
    load_sem, small_sem, x_sem, fs_sem, fr_sem, bs_sem, br_sem,
    gs_sem, gr_sem, hs_sem, hr_sem, zs_sem, zr_sem, ts_sem, tr_sem,
):
    me = lax.axis_index("space")
    row = lax.axis_index("dp")

    my_x, my_zh = me // 4, lax.rem(me, 4)
    my_zl, my_yc = row // 8, lax.rem(row, 8)

    def yc_peer(yc):
        return {"dp": my_zl * 8 + yc}

    def x_peer(x):
        return {"space": x * 4 + my_zh}

    def z_peer(z):
        return {"dp": (z // 4) * 8 + my_yc, "space": my_x * 4 + lax.rem(z, 4)}

    my_z = my_zl * 4 + my_zh
    barrier = pltpu.get_barrier_semaphore()

    def greet(device):
        pl.semaphore_signal(barrier, inc=1, device_id=device, device_id_type=MESH)

    def greet_space(o, carry):
        greet({"space": lax.rem(me + o, G)})
        return carry

    def greet_yc(o, carry):
        greet(yc_peer(lax.rem(my_yc + o, 8)))
        return carry

    def greet_z(o, carry):
        greet(z_peer((1 - my_zl) * 4 + o))
        return carry

    lon_first = pltpu.make_async_copy(lon_hbm.at[0], lon_ref.at[0], load_sem.at[0])
    lon_first.start()
    x_loads = []
    for i in range(4):
        part = pl.ds(6 * i, min(6, HL - 6 * i))
        x_loads.append(
            pltpu.make_async_copy(x_hbm.at[part], x_ref.at[part, pl.ds(0, C)], x_sem.at[i])
        )
        x_loads[-1].start()
    lon_rest = pltpu.make_async_copy(
        lon_hbm.at[pl.ds(1, 5)], lon_ref.at[pl.ds(1, 5)], load_sem.at[1]
    )
    lat_load = pltpu.make_async_copy(lat_hbm, lat_ref, load_sem.at[2])
    y_load = pltpu.make_async_copy(y_hbm, y_ref, load_sem.at[3])
    small = [
        pltpu.make_async_copy(src, dst, small_sem.at[i])
        for i, (src, dst) in enumerate(
            [(w1_hbm, w1_in), (b1_hbm, b1_in), (w2_hbm, w2_in), (b2_hbm, b2_in)]
        )
    ]
    lax.fori_loop(1, G, greet_space, 0)
    lax.fori_loop(1, 8, greet_yc, 0)
    lax.fori_loop(0, 4, greet_z, 0)
    x_ref[:, C:] = jnp.zeros((HP, CP - C, W), BF16)
    x_ref[HL, :C] = jnp.zeros((C, W), BF16)

    lane = lax.broadcasted_iota(jnp.int32, (HP, CP), 1)
    sub = lax.broadcasted_iota(jnp.int32, (HP, CP), 0)
    lane6 = lax.broadcasted_iota(jnp.int32, (6, CP), 1)

    def over_peers(first, body, sign=1, n=G):
        def step(o, c):
            body(lax.rem(first + n + sign * o, n))
            return c

        lax.fori_loop(1, n, step, 0)

    def copies(src, dst, send, recv, c):
        def out(peer):
            return pltpu.make_async_remote_copy(
                src_ref=src[c].at[peer], dst_ref=dst[c].at[me], send_sem=send.at[c, peer],
                recv_sem=recv.at[c, me], device_id={"space": peer}, device_id_type=MESH,
            )

        def arrival(peer):
            return pltpu.make_async_remote_copy(
                src_ref=src[c].at[peer], dst_ref=dst[c].at[peer], send_sem=send.at[c, peer],
                recv_sem=recv.at[c, peer], device_id={"space": peer}, device_id_type=MESH,
            )

        return out, arrival

    forward = [copies(fs, fr, fs_sem, fr_sem, c) for c in range(len(CHUNKS))]
    backward = [copies(bs, br, bs_sem, br_sem, c) for c in range(len(CHUNKS))]

    def longitude(groups):
        size = ROWS * len(groups)

        def two(i, carry):
            pair = x_ref[pl.ds(2 * i, 2)].reshape(2 * CP, W)
            table = lon_ref[groups[0] : groups[0] + len(groups)].reshape(size, W)
            got = nt(table, pair)
            work[pl.ds(pl.multiple_of(2 * i * size, ROWS), size), :] = got[:, :CP]
            work[pl.ds(pl.multiple_of((2 * i + 1) * size, ROWS), size), :] = got[:, CP:]
            return carry

        if groups[0] == 0:
            for i in range(4):
                x_loads[i].wait()
                if i == 3:
                    for load in (lon_rest, lat_load, y_load, *small):
                        load.start()
                lax.fori_loop(3 * i, 3 * i + 3, two, 0)
        else:
            lax.fori_loop(0, HP // 2, two, 0)

    def quarters(load):
        made = load(0)
        for q in range(1, 4):
            made = jnp.where(lane6 < 32 * q, made, load(q))
        return made

    def padded(tiles, extra, first=0):
        done = []
        for t in range(len(tiles[0])):
            both = []
            for s in range(2):
                v = tiles[s][t]
                if extra is not None and first + t < 6:
                    one = jnp.broadcast_to(extra[s][first + t : first + t + 1], (HP, CP))
                    v = jnp.where(sub == HL, one, v)
                both.append(v)
            done.append(jnp.concatenate(both, 0).astype(BF16))
        return done

    def packed(groups, owner):
        size = ROWS * len(groups)
        tiles, extra = [[], []], None
        for i, group in enumerate(groups):
            for s in range(2):
                at = i * ROWS + owner * 2 * KG + s * KG
                a = [work[pl.ds(at + k, HP, stride=size), :] for k in range(KG)]
                r1 = pltpu.roll(a[1], 96, 1)
                r2 = pltpu.roll(a[2], 64, 1)
                tiles[s].append(jnp.where(lane < 96, a[0], r1))
                tiles[s].append(jnp.where(lane < 64, r1, r2))
                if group == ODD:
                    extra = extra or []
                    extra.append(
                        quarters(
                            lambda q, at=at: pltpu.roll(
                                work[pl.ds(at + 2 + 6 * q * size, 6, stride=size), :],
                                (64 + 32 * q) % CP,
                                1,
                            )
                        )
                    )
                else:
                    tiles[s].append(jnp.where(lane < 32, r2, pltpu.roll(a[3], 32, 1)))
        return padded(tiles, extra)

    for c, groups in enumerate(CHUNKS):
        if c == 0:
            lon_first.wait()
        if c == 1:
            lon_rest.wait()
        longitude(groups)
        if c == 0:
            pl.semaphore_wait(barrier, 15 + 7 + 4)

        def send(peers, c=c, groups=groups):
            for peer in peers:
                for t, part in enumerate(packed(groups, peer)):
                    fs[c][peer, :, t * CP : (t + 1) * CP] = part
            for peer in peers:
                forward[c][0](peer).start()

        def send_two(i, carry, send=send):
            send([lax.rem(me + 2 * i, G), lax.rem(me + 2 * i + 1, G)])
            return carry

        send([lax.rem(me + 1, G)])
        lax.fori_loop(1, G // 2, send_two, 0)
        for t, part in enumerate(packed(groups, me)):
            fr[c][me, :, t * CP : (t + 1) * CP] = part

    for load in (lat_load, y_load, *small):
        load.wait()
    eye = lax.broadcasted_iota(jnp.int32, (C, C), 0) == lax.broadcasted_iota(jnp.int32, (C, C), 1)
    eye = eye.astype(F32).astype(BF16)
    for w, b, m_ref, t_ref, bias_ref in (
        (w1_in, b1_in, w1_ref, w1t_ref, b1_ref),
        (w2_in, b2_in, w2_ref, w2t_ref, b2_ref),
    ):
        wr, wi = w[0].astype(F32), w[1].astype(F32)
        wrt, wit = nt(eye, w[0]), nt(eye, w[1])
        m_ref[:C] = jnp.concatenate([wr, wi], 1).astype(BF16)
        m_ref[C:] = jnp.concatenate([-wi, wr], 1).astype(BF16)
        t_ref[:C] = jnp.concatenate([wrt, -wit], 1).astype(BF16)
        t_ref[C:] = jnp.concatenate([wit, wrt], 1).astype(BF16)
        column = nt(eye, b[...])
        bias_ref[:C] = jnp.broadcast_to(column[:, 0:1], (C, PP))
        bias_ref[C:] = jnp.broadcast_to(column[:, 1:2], (C, PP))
    for ref in (gw1, gw2, gb1, gb2, yk_ref):
        ref[...] = jnp.zeros_like(ref)

    def folded(v):
        v = v.astype(F32)
        return v[:, :CP] + v[:, CP : 2 * CP] + v[:, 2 * CP :]

    def mix(group):
        for k in range(COUNT[group]):
            at = BASE[group] + k
            rows = slice(k * C, (k + 1) * C)
            mult = jnp.where(at + me == 0, SCALE, 2.0 * SCALE).astype(F32)
            dzk = jnp.concatenate([dz_ref[rows, :PP], dz_ref[rows, PP:]], 0) * mult
            yk_ref[k, :C, :H] = y_ref[0, at]
            yk_ref[k, C:, :H] = y_ref[1, at]
            yk = yk_ref[k]
            u = nn(w1t_ref[...], yk) + b1_ref[...]
            a = jnp.maximum(u, 0.0).astype(BF16)
            v = nn(w2t_ref[...], a) + b2_ref[...]
            dv = jnp.where(jnp.abs(v) > LAM, dzk, 0.0).astype(BF16)
            gw2[...] += nt(a, dv)
            gb2[...] += folded(dv)
            da = nn(w2_ref[...], dv)
            du = jnp.where(u > 0.0, da, 0.0).astype(BF16)
            gw1[...] += nt(yk, du)
            gb1[...] += folded(du)
            dy = nn(w1_ref[...], du).astype(BF16)
            dy_ref[rows, :PP] = dy[:C]
            dy_ref[rows, PP:] = dy[C:]

    def spread(chunk, g, s, store):
        at = 16 + 16 * s
        v = chunk[g, at : at + 16, : 6 * CP].astype(F32)
        r = HL - 16 if s == 0 else 15
        six = jnp.concatenate([v[r : r + 1, t * CP : (t + 1) * CP] for t in range(6)], 0)
        for q in range(4):
            store(q, six if q == 0 else pltpu.roll(six, CP - 32 * q, 1))

    def middle(c, groups):
        over_peers(me, lambda peer: forward[c][1](peer).wait_recv(), -1)
        if ODD in groups:

            def collect(g, carry):
                for s in range(2):

                    def store(q, v, s=s):
                        rem[pl.ds(g * MSG + s * HP + 6 * q, 6), :] = v

                    spread(fr[c], g, s, store)
                return carry

            lax.fori_loop(0, G, collect, 0)
        lanes = 0
        for group in groups:
            if group == ODD:
                got = fr[c][:, :, : 2 * CP].reshape(G * MSG, 2 * CP)
                got = jnp.concatenate([got, rem[...].astype(BF16)], 1)
            else:
                got = fr[c][:, :, lanes : lanes + PP].reshape(G * MSG, PP)
            dz_ref[...] = tn(got, lat_ref[...])
            mix(group)
            q = nt(lat_ref[...], dy_ref[...])
            width = 2 * CP if group == ODD else PP
            if len(groups) == 1:
                bs[c][...] = q.astype(BF16).reshape(G, MSG, PP)
            else:
                q_ref[...] = q

                def place(g, carry, group=group, lanes=lanes, width=width):
                    tiles, extra = [], []
                    for s in range(2):
                        at = pl.multiple_of(g * MSG + s * HP, 8)
                        v = q_ref[pl.ds(at, HP), :]
                        tiles.append([v[:, t * CP : (t + 1) * CP] for t in range(width // CP)])
                        if group == ODD:

                            def load(q, v=v[:, 2 * CP :]):
                                v = v[6 * q : 6 * q + 6]
                                return v if q == 0 else pltpu.roll(v, 32 * q, 1)

                            pads[g, s, :6] = quarters(load)
                        extra.append(pads[g, s])
                    for t, part in enumerate(padded(tiles, extra, lanes // CP)):
                        bs[c][g, :, lanes + t * CP : lanes + (t + 1) * CP] = part
                    return carry

                lax.fori_loop(0, G, place, 0)
            lanes += width

    def send_back(c):
        over_peers(me, lambda peer: backward[c][0](peer).start())
        br[c][me] = bs[c][me]

    for c in range(3):
        middle(c, CHUNKS[c])
        send_back(c)
    middle(3, CHUNKS[3])

    def combined(g):
        re = g[:C, :C] + g[C:, C:]
        im = g[:C, C:] - g[C:, :C]
        return re, im

    sums = []
    for g, b in ((gw1, gb1), (gw2, gb2)):
        total = jnp.sum(b[...], axis=1, keepdims=True)
        for part, bias in zip(combined(g[...]), (total[:C], total[C:])):
            wide = jnp.concatenate([part, jnp.broadcast_to(bias, (C, CP - C))], 1)
            sums.append(wide)
    zero2 = jnp.zeros((2, CP), F32)
    for d in range(G):
        for i, v in enumerate(sums):
            gs[d % 8, d // 8, 8 * i : 8 * i + 8] = jnp.concatenate([v[6 * d : 6 * d + 6], zero2], 0)

    def yc_copy(peer, at):
        return pltpu.make_async_remote_copy(
            src_ref=gs.at[peer], dst_ref=gr.at[at], send_sem=gs_sem.at[peer],
            recv_sem=gr_sem.at[at], device_id=yc_peer(peer), device_id_type=MESH,
        )

    def x_copy(peer, at):
        return pltpu.make_async_remote_copy(
            src_ref=hs.at[peer], dst_ref=hr.at[at], send_sem=hs_sem.at[peer],
            recv_sem=hr_sem.at[at], device_id=x_peer(peer), device_id_type=MESH,
        )

    def z_copy(peer, at):
        return pltpu.make_async_remote_copy(
            src_ref=zs.at[peer // 4], dst_ref=zr.at[at], send_sem=zs_sem.at[peer],
            recv_sem=zr_sem.at[at], device_id=z_peer(peer), device_id_type=MESH,
        )

    def share_copy(peer, at):
        return pltpu.make_async_remote_copy(
            src_ref=ts, dst_ref=tr.at[at], send_sem=ts_sem.at[peer],
            recv_sem=tr_sem.at[at], device_id=x_peer(peer), device_id_type=MESH,
        )

    over_peers(my_yc, lambda peer: yc_copy(peer, my_yc).start(), 1, 8)
    gr[my_yc] = gs[my_yc]
    over_peers(my_yc, lambda peer: yc_copy(peer, peer).wait_recv(), -1, 8)
    total = jnp.sum(gr[...], axis=0)
    for x in range(4):
        hs[x] = total[:, 8 * x : 8 * x + 8]
    over_peers(my_x, lambda peer: x_copy(peer, my_x).start(), 1, 4)
    hr[my_x] = hs[my_x]
    over_peers(my_x, lambda peer: x_copy(peer, peer).wait_recv(), -1, 4)
    zs[...] = jnp.sum(hr[...], axis=0)
    over_peers(my_z, lambda peer: z_copy(peer, my_z).start(), 1, 8)
    zr[my_z] = zs[my_zl]
    send_back(3)

    def finish(chunks, between=None):
        groups = [group for c in chunks for group in CHUNKS[c]]
        size = ROWS * len(groups)

        def unpack(c, g):
            lanes = 0
            for group in CHUNKS[c]:
                i = groups.index(group)
                width = 2 * CP if group == ODD else PP
                got = br[c][g, :, lanes : lanes + width].astype(F32)
                for s in range(2):
                    p = [
                        got[s * HP : (s + 1) * HP, t * CP : (t + 1) * CP]
                        for t in range(width // CP)
                    ]
                    parts = [
                        p[0],
                        jnp.where(lane < 32, pltpu.roll(p[0], 32, 1), pltpu.roll(p[1], 32, 1)),
                    ]
                    if group == ODD:

                        def store(q, v, s=s):
                            few[s, 6 * q : 6 * q + 6, :] = v

                        spread(br[c], g, s, store)
                        last = few[s]
                    else:
                        last = p[2]
                    parts.append(
                        jnp.where(lane < 64, pltpu.roll(p[1], 64, 1), pltpu.roll(last, 64, 1))
                    )
                    if group == ODD:
                        parts.append(jnp.zeros((HP, CP), F32))
                    else:
                        parts.append(pltpu.roll(last, 96, 1))
                    for k in range(KG):
                        at = i * ROWS + g * 2 * KG + s * KG + k
                        work[pl.ds(at, HP, stride=size), :] = parts[k]
                lanes += width

        def arrive(c):
            def two(i, carry):
                peers = [lax.rem(me + G - 2 * i, G), lax.rem(me + G - 2 * i - 1, G)]
                for peer in peers:
                    backward[c][1](peer).wait_recv()
                for peer in peers:
                    unpack(c, peer)
                return carry

            first = lax.rem(me + G - 1, G)
            backward[c][1](first).wait_recv()
            unpack(c, me)
            unpack(c, first)
            lax.fori_loop(1, G // 2, two, 0)

        for c in chunks:
            arrive(c)
            if between is not None and c == chunks[0]:
                between()
        table = lon_ref[groups[0] : groups[0] + len(groups)].reshape(size, W)

        def block(first, count):
            columns = []
            for i in range(count):
                v = work[pl.ds(pl.multiple_of((first + i) * size, ROWS), size), :].astype(BF16)
                columns.append(jnp.transpose(v)[:C])
            new = nn(jnp.concatenate(columns, 0), table).reshape(count, C, W) * SCALE
            at = pl.ds(first, count)
            if chunks[0] == 0:
                acc[at] = x_ref[at, :C].astype(F32) + new
            elif chunks[-1] < len(CHUNKS) - 1:
                acc[at] += new
            else:
                out_ref[at] = (acc[at] + new).astype(BF16)

        def four(i, carry):
            block(4 * i, 4)
            return carry

        lax.fori_loop(0, HL // 4, four, 0)
        block(HL // 4 * 4, HL % 4)

    for c in range(len(CHUNKS)):
        over_peers(me, lambda peer, c=c: forward[c][0](peer).wait_send())
    over_peers(my_yc, lambda peer: yc_copy(peer, my_yc).wait_send(), 1, 8)
    over_peers(my_x, lambda peer: x_copy(peer, my_x).wait_send(), 1, 4)
    def share():
        over_peers(my_z, lambda peer: z_copy(peer, peer).wait_recv(), -1, 8)
        ts[...] = jnp.sum(zr[...], axis=0)
        over_peers(my_x, lambda peer: share_copy(peer, my_x).start(), 1, 4)
        tr[my_x] = ts[...]

    finish((0,))
    finish((1,))
    for c in range(2):
        over_peers(me, lambda peer, c=c: backward[c][0](peer).wait_send())
    finish((2, 3), share)
    over_peers(my_x, lambda peer: share_copy(peer, peer).wait_recv(), -1, 4)
    g_ref[...] = tr[...]
    for c in range(2, 4):
        over_peers(me, lambda peer, c=c: backward[c][0](peer).wait_send())
    over_peers(my_z, lambda peer: z_copy(peer, my_z).wait_send(), 1, 8)
    over_peers(my_x, lambda peer: share_copy(peer, my_x).wait_send(), 1, 4)


def emit(g_in, gw1_ref, gb1_ref, gw2_ref, gb2_ref):
    rows = lax.broadcasted_iota(jnp.int32, (8, CP), 0)
    lanes = lax.broadcasted_iota(jnp.int32, (8, CP), 1)
    for i, (w_ref, b_ref) in enumerate(((gw1_ref, gb1_ref), (gw2_ref, gb2_ref))):
        for s in range(2):
            v = g_in[2 * i + s]
            for r in range(6):
                w_ref[s, r, :, :] = v[r : r + 1, :C]
            spread = jnp.where(rows == lanes, jnp.broadcast_to(v[:, C : C + 1], (8, CP)), 0.0)
            b_ref[s, :, :] = jnp.sum(spread, axis=0, keepdims=True)[:, :6]


def on_device(cotangent, spectrum, first_weight, first_bias, second_weight, second_bias):
    x = jnp.transpose(cotangent[0], (1, 0, 2))
    y = jnp.transpose(spectrum[0], (0, 2, 1, 3))
    any_spec = pl.BlockSpec(memory_space=pl.ANY)
    vmem = pl.BlockSpec(memory_space=pltpu.VMEM)
    dma = pltpu.SemaphoreType.DMA
    messages = [pltpu.VMEM((G, MSG, lanes), BF16) for lanes in LANES]
    n = len(CHUNKS)
    out, g = pl.pallas_call(
        kernel,
        out_shape=(
            pltpu.VMEM((HL, C, W), BF16),
            pltpu.VMEM((4, 8, CP), F32),
        ),
        in_specs=[any_spec] * 8,
        out_specs=(vmem, vmem),
        scratch_shapes=[
            pltpu.VMEM((2, C, C), BF16),
            pltpu.VMEM((2, C), BF16),
            pltpu.VMEM((2, C, C), BF16),
            pltpu.VMEM((2, C), BF16),
            pltpu.VMEM((HP, CP, W), BF16),
            pltpu.VMEM((2, HL, C, H), BF16),
            pltpu.VMEM((len(BASE), ROWS, W), BF16),
            pltpu.VMEM((G * MSG, 2 * PP), BF16),
            messages,
            messages,
            messages,
            messages,
            pltpu.VMEM((HP * MOST * ROWS, CP), F32),
            pltpu.VMEM((HL, C, W), F32),
            pltpu.VMEM((KG * C, 2 * PP), F32),
            pltpu.VMEM((KG * C, 2 * PP), BF16),
            pltpu.VMEM((G * MSG, PP), F32),
            pltpu.VMEM((G * MSG, CP), F32),
            pltpu.VMEM((G, 2, 8, CP), F32),
            pltpu.VMEM((2, HP, CP), F32),
            pltpu.VMEM((KG, 2 * C, PP), BF16),
            pltpu.VMEM((2 * C, 2 * C), BF16),
            pltpu.VMEM((2 * C, 2 * C), BF16),
            pltpu.VMEM((2 * C, 2 * C), BF16),
            pltpu.VMEM((2 * C, 2 * C), BF16),
            pltpu.VMEM((2 * C, PP), F32),
            pltpu.VMEM((2 * C, PP), F32),
            pltpu.VMEM((2 * C, 2 * C), F32),
            pltpu.VMEM((2 * C, 2 * C), F32),
            pltpu.VMEM((2 * C, CP), F32),
            pltpu.VMEM((2 * C, CP), F32),
            pltpu.VMEM((8, 2, 32, CP), F32),
            pltpu.VMEM((8, 2, 32, CP), F32),
            pltpu.VMEM((4, 2, 8, CP), F32),
            pltpu.VMEM((4, 2, 8, CP), F32),
            pltpu.VMEM((2, 8, CP), F32),
            pltpu.VMEM((8, 8, CP), F32),
            pltpu.VMEM((8, CP), F32),
            pltpu.VMEM((4, 8, CP), F32),
            dma((4,)),
            dma((4,)),
            dma((4,)),
            dma((n, G)),
            dma((n, G)),
            dma((n, G)),
            dma((n, G)),
            dma((8,)),
            dma((8,)),
            dma((4,)),
            dma((4,)),
            dma((8,)),
            dma((8,)),
            dma((4,)),
            dma((4,)),
        ],
        compiler_params=pltpu.CompilerParams(
            collective_id=0, has_side_effects=True, vmem_limit_bytes=52 * 1024 * 1024
        ),
        name="afno_backward",
    )(
        x, y, jnp.asarray(lon_table()), jnp.asarray(lat_table()),
        first_weight[:, 0], first_bias[:, 0], second_weight[:, 0], second_bias[:, 0],
    )
    gw1, gb1, gw2, gb2 = pl.pallas_call(
        emit,
        out_shape=(
            jax.ShapeDtypeStruct((2, 6, 1, C), F32),
            jax.ShapeDtypeStruct((2, 1, 6), F32),
            jax.ShapeDtypeStruct((2, 6, 1, C), F32),
            jax.ShapeDtypeStruct((2, 1, 6), F32),
        ),
        in_specs=[vmem],
        out_specs=(vmem, vmem, vmem, vmem),
        name="emit",
    )(pltpu.with_memory_space_constraint(g, pltpu.VMEM))
    grad_in = jnp.transpose(out, (1, 0, 2))[None]
    gw1, gw2 = [jnp.transpose(v, (0, 2, 1, 3)) for v in (gw1, gw2)]
    return (grad_in, gw1, gb1, gw2, gb2)


def solution(mesh):
    in_specs = (
        P("dp", None, "space", None),
        P("dp", None, None, "space", None),
        P(),
        P(),
        P(),
        P(),
    )
    out_specs = (
        P("dp", None, "space", None),
        P(None, None, "dp", None),
        P(None, None, "dp"),
        P(None, None, "dp", None),
        P(None, None, "dp"),
    )
    return jax.shard_map(
        on_device, mesh=mesh, in_specs=in_specs, out_specs=out_specs, check_vma=False
    )
```

```python
import math

import jax
import jax.numpy as jnp
import ml_dtypes
import numpy as np
from jax import lax
from jax.experimental import pallas as pl
from jax.experimental.pallas import tpu as pltpu
from jax.sharding import PartitionSpec as P

H = 368
W = 768
KW = 368
C = 96
G = 16
HL = 23
HP = 24
CP = 128
KG = 4
ROWS = G * 2 * KG
BASE = (0, 4, 7, 11, 15, 19)
COUNT = (4, 3, 4, 4, 4, 4)
ODD = 1
CHUNKS = ((0,), (1, 2, 3), (4,), (5,))
LANES = (384, 1024, 384, 384)
MOST = 3
MSG = 2 * HP
PP = 384
SCALE = 1.0 / math.sqrt(H * W)
LAM = 0.01
F32 = jnp.float32
BF16 = jnp.bfloat16
MESH = pl.DeviceIdType.MESH


def angles(n, rows, cols):
    index = (rows[:, None].astype(np.int64) * cols[None, :].astype(np.int64)) % n
    theta = index.astype(np.float32) * np.float32(2.0 * math.pi / n)
    return np.cos(theta), np.sin(theta)


def lon_table():
    cos, sin = angles(W, np.arange(KW), np.arange(W))
    both = np.stack([cos, -sin], 1).reshape(G, HL, 2, W).transpose(0, 2, 1, 3)
    full = np.zeros((len(BASE), G, 2, KG, W), np.float32)
    for i, (base, count) in enumerate(zip(BASE, COUNT)):
        full[i, :, :, :count] = both[:, :, base : base + count]
    return full.reshape(len(BASE), ROWS, W).astype(ml_dtypes.bfloat16)


def lat_table():
    cos, sin = angles(H, np.arange(H), np.arange(H))
    full = np.zeros((G, 2, HP, 2, PP), np.float32)
    cos, sin = cos.reshape(G, HL, H), sin.reshape(G, HL, H)
    full[:, 0, :HL, 0, :H] = cos
    full[:, 1, :HL, 0, :H] = sin
    full[:, 0, :HL, 1, :H] = -sin
    full[:, 1, :HL, 1, :H] = cos
    return full.reshape(G * MSG, 2 * PP).astype(ml_dtypes.bfloat16)


def nt(a, b):
    return lax.dot_general(a, b, (((1,), (1,)), ((), ())), preferred_element_type=F32)


def tn(a, b):
    return lax.dot_general(a, b, (((0,), (0,)), ((), ())), preferred_element_type=F32)


def nn(a, b):
    return jnp.dot(a, b, preferred_element_type=F32)


def kernel(
    x_hbm, y_hbm, lon_hbm, lat_hbm, w1_hbm, b1_hbm, w2_hbm, b2_hbm,
    out_ref, g_ref,
    w1_in, b1_in, w2_in, b2_in, x_ref, y_ref, lon_ref, lat_ref, fs, fr, bs, br, work, acc, dz_ref, dy_ref, q_ref, rem, pads, few,
    yk_ref, w1t_ref, w1_ref, w2t_ref, w2_ref, b1_ref, b2_ref, gw1, gw2, gb1, gb2,
    gs, gr, hs, hr, zs, zr, ts, tr,
    load_sem, small_sem, x_sem, fs_sem, fr_sem, bs_sem, br_sem,
    gs_sem, gr_sem, hs_sem, hr_sem, zs_sem, zr_sem, ts_sem, tr_sem,
):
    me = lax.axis_index("space")
    row = lax.axis_index("dp")

    my_x, my_zh = me // 4, lax.rem(me, 4)
    my_zl, my_yc = row // 8, lax.rem(row, 8)

    def yc_peer(yc):
        return {"dp": my_zl * 8 + yc}

    def x_peer(x):
        return {"space": x * 4 + my_zh}

    def z_peer(z):
        return {"dp": (z // 4) * 8 + my_yc, "space": my_x * 4 + lax.rem(z, 4)}

    my_z = my_zl * 4 + my_zh
    barrier = pltpu.get_barrier_semaphore()

    def greet(device):
        pl.semaphore_signal(barrier, inc=1, device_id=device, device_id_type=MESH)

    def greet_space(o, carry):
        greet({"space": lax.rem(me + o, G)})
        return carry

    def greet_yc(o, carry):
        greet(yc_peer(lax.rem(my_yc + o, 8)))
        return carry

    def greet_z(o, carry):
        greet(z_peer((1 - my_zl) * 4 + o))
        return carry

    lon_first = pltpu.make_async_copy(lon_hbm.at[0], lon_ref.at[0], load_sem.at[0])
    lon_first.start()
    x_loads = []
    for i in range(4):
        part = pl.ds(6 * i, min(6, HL - 6 * i))
        x_loads.append(
            pltpu.make_async_copy(x_hbm.at[part], x_ref.at[part, pl.ds(0, C)], x_sem.at[i])
        )
        x_loads[-1].start()
    lon_rest = pltpu.make_async_copy(
        lon_hbm.at[pl.ds(1, 5)], lon_ref.at[pl.ds(1, 5)], load_sem.at[1]
    )
    lat_load = pltpu.make_async_copy(lat_hbm, lat_ref, load_sem.at[2])
    y_load = pltpu.make_async_copy(y_hbm, y_ref, load_sem.at[3])
    small = [
        pltpu.make_async_copy(src, dst, small_sem.at[i])
        for i, (src, dst) in enumerate(
            [(w1_hbm, w1_in), (b1_hbm, b1_in), (w2_hbm, w2_in), (b2_hbm, b2_in)]
        )
    ]
    lax.fori_loop(1, G, greet_space, 0)
    lax.fori_loop(1, 8, greet_yc, 0)
    lax.fori_loop(0, 4, greet_z, 0)
    x_ref[:, C:] = jnp.zeros((HP, CP - C, W), BF16)
    x_ref[HL, :C] = jnp.zeros((C, W), BF16)

    lane = lax.broadcasted_iota(jnp.int32, (HP, CP), 1)
    sub = lax.broadcasted_iota(jnp.int32, (HP, CP), 0)
    lane6 = lax.broadcasted_iota(jnp.int32, (6, CP), 1)

    def over_peers(first, body, sign=1, n=G):
        def step(o, c):
            body(lax.rem(first + n + sign * o, n))
            return c

        lax.fori_loop(1, n, step, 0)

    def copies(src, dst, send, recv, c):
        def out(peer):
            return pltpu.make_async_remote_copy(
                src_ref=src[c].at[peer], dst_ref=dst[c].at[me], send_sem=send.at[c, peer],
                recv_sem=recv.at[c, me], device_id={"space": peer}, device_id_type=MESH,
            )

        def arrival(peer):
            return pltpu.make_async_remote_copy(
                src_ref=src[c].at[peer], dst_ref=dst[c].at[peer], send_sem=send.at[c, peer],
                recv_sem=recv.at[c, peer], device_id={"space": peer}, device_id_type=MESH,
            )

        return out, arrival

    forward = [copies(fs, fr, fs_sem, fr_sem, c) for c in range(len(CHUNKS))]
    backward = [copies(bs, br, bs_sem, br_sem, c) for c in range(len(CHUNKS))]

    def longitude(groups):
        size = ROWS * len(groups)

        def two(i, carry):
            pair = x_ref[pl.ds(2 * i, 2)].reshape(2 * CP, W)
            table = lon_ref[groups[0] : groups[0] + len(groups)].reshape(size, W)
            got = nt(table, pair)
            work[pl.ds(pl.multiple_of(2 * i * size, ROWS), size), :] = got[:, :CP]
            work[pl.ds(pl.multiple_of((2 * i + 1) * size, ROWS), size), :] = got[:, CP:]
            return carry

        if groups[0] == 0:
            for i in range(4):
                x_loads[i].wait()
                if i == 3:
                    for load in (lon_rest, lat_load, y_load, *small):
                        load.start()
                lax.fori_loop(3 * i, 3 * i + 3, two, 0)
        else:
            lax.fori_loop(0, HP // 2, two, 0)

    def quarters(load):
        made = load(0)
        for q in range(1, 4):
            made = jnp.where(lane6 < 32 * q, made, load(q))
        return made

    def padded(tiles, extra, first=0):
        done = []
        for t in range(len(tiles[0])):
            both = []
            for s in range(2):
                v = tiles[s][t]
                if extra is not None and first + t < 6:
                    one = jnp.broadcast_to(extra[s][first + t : first + t + 1], (HP, CP))
                    v = jnp.where(sub == HL, one, v)
                both.append(v)
            done.append(jnp.concatenate(both, 0).astype(BF16))
        return done

    def packed(groups, owner):
        size = ROWS * len(groups)
        tiles, extra = [[], []], None
        for i, group in enumerate(groups):
            for s in range(2):
                at = i * ROWS + owner * 2 * KG + s * KG
                a = [work[pl.ds(at + k, HP, stride=size), :] for k in range(KG)]
                r1 = pltpu.roll(a[1], 96, 1)
                r2 = pltpu.roll(a[2], 64, 1)
                tiles[s].append(jnp.where(lane < 96, a[0], r1))
                tiles[s].append(jnp.where(lane < 64, r1, r2))
                if group == ODD:
                    extra = extra or []
                    extra.append(
                        quarters(
                            lambda q, at=at: pltpu.roll(
                                work[pl.ds(at + 2 + 6 * q * size, 6, stride=size), :],
                                (64 + 32 * q) % CP,
                                1,
                            )
                        )
                    )
                else:
                    tiles[s].append(jnp.where(lane < 32, r2, pltpu.roll(a[3], 32, 1)))
        return padded(tiles, extra)

    for c, groups in enumerate(CHUNKS):
        if c == 0:
            lon_first.wait()
        if c == 1:
            lon_rest.wait()
        longitude(groups)
        if c == 0:
            pl.semaphore_wait(barrier, 15 + 7 + 4)

        def send(peers, c=c, groups=groups):
            for peer in peers:
                for t, part in enumerate(packed(groups, peer)):
                    fs[c][peer, :, t * CP : (t + 1) * CP] = part
            for peer in peers:
                forward[c][0](peer).start()

        def send_two(i, carry, send=send):
            send([lax.rem(me + 2 * i, G), lax.rem(me + 2 * i + 1, G)])
            return carry

        send([lax.rem(me + 1, G)])
        lax.fori_loop(1, G // 2, send_two, 0)
        for t, part in enumerate(packed(groups, me)):
            fr[c][me, :, t * CP : (t + 1) * CP] = part

    for load in (lat_load, y_load, *small):
        load.wait()
    eye = lax.broadcasted_iota(jnp.int32, (C, C), 0) == lax.broadcasted_iota(jnp.int32, (C, C), 1)
    eye = eye.astype(F32).astype(BF16)
    for w, b, m_ref, t_ref, bias_ref in (
        (w1_in, b1_in, w1_ref, w1t_ref, b1_ref),
        (w2_in, b2_in, w2_ref, w2t_ref, b2_ref),
    ):
        wr, wi = w[0].astype(F32), w[1].astype(F32)
        wrt, wit = nt(eye, w[0]), nt(eye, w[1])
        m_ref[:C] = jnp.concatenate([wr, wi], 1).astype(BF16)
        m_ref[C:] = jnp.concatenate([-wi, wr], 1).astype(BF16)
        t_ref[:C] = jnp.concatenate([wrt, -wit], 1).astype(BF16)
        t_ref[C:] = jnp.concatenate([wit, wrt], 1).astype(BF16)
        column = nt(eye, b[...])
        bias_ref[:C] = jnp.broadcast_to(column[:, 0:1], (C, PP))
        bias_ref[C:] = jnp.broadcast_to(column[:, 1:2], (C, PP))
    for ref in (gw1, gw2, gb1, gb2, yk_ref):
        ref[...] = jnp.zeros_like(ref)

    def folded(v):
        v = v.astype(F32)
        return v[:, :CP] + v[:, CP : 2 * CP] + v[:, 2 * CP :]

    def mix(group):
        for k in range(COUNT[group]):
            at = BASE[group] + k
            rows = slice(k * C, (k + 1) * C)
            mult = jnp.where(at + me == 0, SCALE, 2.0 * SCALE).astype(F32)
            dzk = jnp.concatenate([dz_ref[rows, :PP], dz_ref[rows, PP:]], 0) * mult
            yk_ref[k, :C, :H] = y_ref[0, at]
            yk_ref[k, C:, :H] = y_ref[1, at]
            yk = yk_ref[k]
            u = nn(w1t_ref[...], yk) + b1_ref[...]
            a = jnp.maximum(u, 0.0).astype(BF16)
            v = nn(w2t_ref[...], a) + b2_ref[...]
            dv = jnp.where(jnp.abs(v) > LAM, dzk, 0.0).astype(BF16)
            gw2[...] += nt(a, dv)
            gb2[...] += folded(dv)
            da = nn(w2_ref[...], dv)
            du = jnp.where(u > 0.0, da, 0.0).astype(BF16)
            gw1[...] += nt(yk, du)
            gb1[...] += folded(du)
            dy = nn(w1_ref[...], du).astype(BF16)
            dy_ref[rows, :PP] = dy[:C]
            dy_ref[rows, PP:] = dy[C:]

    def spread(chunk, g, s, store):
        at = 16 + 16 * s
        v = chunk[g, at : at + 16, : 6 * CP].astype(F32)
        r = HL - 16 if s == 0 else 15
        six = jnp.concatenate([v[r : r + 1, t * CP : (t + 1) * CP] for t in range(6)], 0)
        for q in range(4):
            store(q, six if q == 0 else pltpu.roll(six, CP - 32 * q, 1))

    def middle(c, groups):
        over_peers(me, lambda peer: forward[c][1](peer).wait_recv(), -1)
        if ODD in groups:

            def collect(g, carry):
                for s in range(2):

                    def store(q, v, s=s):
                        rem[pl.ds(g * MSG + s * HP + 6 * q, 6), :] = v

                    spread(fr[c], g, s, store)
                return carry

            lax.fori_loop(0, G, collect, 0)
        lanes = 0
        for group in groups:
            if group == ODD:
                got = fr[c][:, :, : 2 * CP].reshape(G * MSG, 2 * CP)
                got = jnp.concatenate([got, rem[: G * MSG].astype(BF16)], 1)
            else:
                got = fr[c][:, :, lanes : lanes + PP].reshape(G * MSG, PP)
            dz_ref[...] = tn(got, lat_ref[...])
            mix(group)
            q = nt(lat_ref[...], dy_ref[...])
            width = 2 * CP if group == ODD else PP
            if len(groups) == 1:
                bs[c][...] = q.astype(BF16).reshape(G, MSG, PP)
            else:
                q_ref[...] = q

                def place(g, carry, group=group, lanes=lanes, width=width):
                    tiles, extra = [], []
                    for s in range(2):
                        at = pl.multiple_of(g * MSG + s * HP, 8)
                        v = q_ref[pl.ds(at, HP), :]
                        tiles.append([v[:, t * CP : (t + 1) * CP] for t in range(width // CP)])
                        if group == ODD:

                            def load(q, v=v[:, 2 * CP :]):
                                v = v[6 * q : 6 * q + 6]
                                return v if q == 0 else pltpu.roll(v, 32 * q, 1)

                            pads[g, s, :6] = quarters(load)
                        extra.append(pads[g, s])
                    for t, part in enumerate(padded(tiles, extra, lanes // CP)):
                        bs[c][g, :, lanes + t * CP : lanes + (t + 1) * CP] = part
                    return carry

                lax.fori_loop(0, G, place, 0)
            lanes += width

    def send_back(c):
        over_peers(me, lambda peer: backward[c][0](peer).start())
        br[c][me] = bs[c][me]

    for c in range(3):
        middle(c, CHUNKS[c])
        send_back(c)
    middle(3, CHUNKS[3])

    def combined(g):
        re = g[:C, :C] + g[C:, C:]
        im = g[:C, C:] - g[C:, :C]
        return re, im

    sums = []
    for g, b in ((gw1, gb1), (gw2, gb2)):
        total = jnp.sum(b[...], axis=1, keepdims=True)
        for part, bias in zip(combined(g[...]), (total[:C], total[C:])):
            wide = jnp.concatenate([part, jnp.broadcast_to(bias, (C, CP - C))], 1)
            sums.append(wide)
    zero2 = jnp.zeros((2, CP), F32)
    for d in range(G):
        for i, v in enumerate(sums):
            gs[d % 8, d // 8, 8 * i : 8 * i + 8] = jnp.concatenate([v[6 * d : 6 * d + 6], zero2], 0)

    def yc_copy(peer, at):
        return pltpu.make_async_remote_copy(
            src_ref=gs.at[peer], dst_ref=gr.at[at], send_sem=gs_sem.at[peer],
            recv_sem=gr_sem.at[at], device_id=yc_peer(peer), device_id_type=MESH,
        )

    def x_copy(peer, at):
        return pltpu.make_async_remote_copy(
            src_ref=hs.at[peer], dst_ref=hr.at[at], send_sem=hs_sem.at[peer],
            recv_sem=hr_sem.at[at], device_id=x_peer(peer), device_id_type=MESH,
        )

    def z_copy(peer, at):
        return pltpu.make_async_remote_copy(
            src_ref=zs.at[peer // 4], dst_ref=zr.at[at], send_sem=zs_sem.at[peer],
            recv_sem=zr_sem.at[at], device_id=z_peer(peer), device_id_type=MESH,
        )

    def share_copy(peer, at):
        return pltpu.make_async_remote_copy(
            src_ref=ts, dst_ref=tr.at[at], send_sem=ts_sem.at[peer],
            recv_sem=tr_sem.at[at], device_id=x_peer(peer), device_id_type=MESH,
        )

    over_peers(my_yc, lambda peer: yc_copy(peer, my_yc).start(), 1, 8)
    gr[my_yc] = gs[my_yc]
    over_peers(my_yc, lambda peer: yc_copy(peer, peer).wait_recv(), -1, 8)
    total = jnp.sum(gr[...], axis=0)
    for x in range(4):
        hs[x] = total[:, 8 * x : 8 * x + 8]
    over_peers(my_x, lambda peer: x_copy(peer, my_x).start(), 1, 4)
    hr[my_x] = hs[my_x]
    over_peers(my_x, lambda peer: x_copy(peer, peer).wait_recv(), -1, 4)
    zs[...] = jnp.sum(hr[...], axis=0)
    over_peers(my_z, lambda peer: z_copy(peer, my_z).start(), 1, 8)
    zr[my_z] = zs[my_zl]
    send_back(3)

    def finish(chunks, between=None):
        groups = [group for c in chunks for group in CHUNKS[c]]
        size = ROWS * len(groups)

        def unpack(c, g):
            lanes = 0
            for group in CHUNKS[c]:
                i = groups.index(group)
                width = 2 * CP if group == ODD else PP
                got = br[c][g, :, lanes : lanes + width].astype(F32)
                for s in range(2):
                    p = [
                        got[s * HP : (s + 1) * HP, t * CP : (t + 1) * CP]
                        for t in range(width // CP)
                    ]
                    parts = [
                        p[0],
                        jnp.where(lane < 32, pltpu.roll(p[0], 32, 1), pltpu.roll(p[1], 32, 1)),
                    ]
                    if group == ODD:

                        def store(q, v, s=s):
                            few[s, 6 * q : 6 * q + 6, :] = v

                        spread(br[c], g, s, store)
                        last = few[s, :HP]
                    else:
                        last = p[2]
                    parts.append(
                        jnp.where(lane < 64, pltpu.roll(p[1], 64, 1), pltpu.roll(last, 64, 1))
                    )
                    if group == ODD:
                        parts.append(jnp.zeros((HP, CP), F32))
                    else:
                        parts.append(pltpu.roll(last, 96, 1))
                    for k in range(KG):
                        at = i * ROWS + g * 2 * KG + s * KG + k
                        work[pl.ds(at, HP, stride=size), :] = parts[k]
                lanes += width

        def arrive(c):
            def two(i, carry):
                peers = [lax.rem(me + G - 2 * i, G), lax.rem(me + G - 2 * i - 1, G)]
                for peer in peers:
                    backward[c][1](peer).wait_recv()
                for peer in peers:
                    unpack(c, peer)
                return carry

            first = lax.rem(me + G - 1, G)
            backward[c][1](first).wait_recv()
            unpack(c, me)
            unpack(c, first)
            lax.fori_loop(1, G // 2, two, 0)

        for c in chunks:
            arrive(c)
            if between is not None and c == chunks[0]:
                between()
        table = lon_ref[groups[0] : groups[0] + len(groups)].reshape(size, W)

        def block(first, count):
            columns = []
            for i in range(count):
                v = work[pl.ds(pl.multiple_of((first + i) * size, ROWS), size), :].astype(BF16)
                columns.append(jnp.transpose(v)[:C])
            new = nn(jnp.concatenate(columns, 0), table).reshape(count, C, W) * SCALE
            at = pl.ds(first, count)
            if chunks[0] == 0:
                acc[at] = x_ref[at, :C].astype(F32) + new
            elif chunks[-1] < len(CHUNKS) - 1:
                acc[at] += new
            else:
                out_ref[at] = (acc[at] + new).astype(BF16)

        def four(i, carry):
            block(4 * i, 4)
            return carry

        lax.fori_loop(0, HL // 4, four, 0)
        block(HL // 4 * 4, HL % 4)

    for c in range(len(CHUNKS)):
        over_peers(me, lambda peer, c=c: forward[c][0](peer).wait_send())
    over_peers(my_yc, lambda peer: yc_copy(peer, my_yc).wait_send(), 1, 8)
    over_peers(my_x, lambda peer: x_copy(peer, my_x).wait_send(), 1, 4)
    def share():
        over_peers(my_z, lambda peer: z_copy(peer, peer).wait_recv(), -1, 8)
        ts[...] = jnp.sum(zr[...], axis=0)
        over_peers(my_x, lambda peer: share_copy(peer, my_x).start(), 1, 4)
        tr[my_x] = ts[...]

    finish((0,))
    finish((1,))
    for c in range(2):
        over_peers(me, lambda peer, c=c: backward[c][0](peer).wait_send())
    finish((2, 3), share)
    over_peers(my_x, lambda peer: share_copy(peer, peer).wait_recv(), -1, 4)
    g_ref[...] = tr[...]
    for c in range(2, 4):
        over_peers(me, lambda peer, c=c: backward[c][0](peer).wait_send())
    over_peers(my_z, lambda peer: z_copy(peer, my_z).wait_send(), 1, 8)
    over_peers(my_x, lambda peer: share_copy(peer, my_x).wait_send(), 1, 4)


def emit(g_in, gw1_ref, gb1_ref, gw2_ref, gb2_ref):
    rows = lax.broadcasted_iota(jnp.int32, (8, CP), 0)
    lanes = lax.broadcasted_iota(jnp.int32, (8, CP), 1)
    for i, (w_ref, b_ref) in enumerate(((gw1_ref, gb1_ref), (gw2_ref, gb2_ref))):
        for s in range(2):
            v = g_in[2 * i + s]
            for r in range(6):
                w_ref[s, r, :, :] = v[r : r + 1, :C]
            spread = jnp.where(rows == lanes, jnp.broadcast_to(v[:, C : C + 1], (8, CP)), 0.0)
            b_ref[s, :, :] = jnp.sum(spread, axis=0, keepdims=True)[:, :6]


def on_device(cotangent, spectrum, first_weight, first_bias, second_weight, second_bias):
    x = jnp.transpose(cotangent[0], (1, 0, 2))
    y = jnp.transpose(spectrum[0], (0, 2, 1, 3))
    any_spec = pl.BlockSpec(memory_space=pl.ANY)
    vmem = pl.BlockSpec(memory_space=pltpu.VMEM)
    dma = pltpu.SemaphoreType.DMA
    messages = [pltpu.VMEM((G, MSG, lanes), BF16) for lanes in LANES]
    n = len(CHUNKS)
    out, g = pl.pallas_call(
        kernel,
        out_shape=(
            pltpu.VMEM((HL, C, W), BF16),
            pltpu.VMEM((4, 8, CP), F32),
        ),
        in_specs=[any_spec] * 8,
        out_specs=(vmem, vmem),
        scratch_shapes=[
            pltpu.VMEM((2, C, C), BF16),
            pltpu.VMEM((2, C), BF16),
            pltpu.VMEM((2, C, C), BF16),
            pltpu.VMEM((2, C), BF16),
            pltpu.VMEM((HP, CP, W), BF16),
            pltpu.VMEM((2, HL, C, H), BF16),
            pltpu.VMEM((len(BASE), ROWS, W), BF16),
            pltpu.VMEM((G * MSG, 2 * PP), BF16),
            messages,
            messages,
            messages,
            messages,
            pltpu.VMEM(((HP + 2) * MOST * ROWS, CP), F32),
            pltpu.VMEM((HL, C, W), F32),
            pltpu.VMEM((KG * C, 2 * PP), F32),
            pltpu.VMEM((KG * C, 2 * PP), BF16),
            pltpu.VMEM((G * MSG, PP), F32),
            pltpu.VMEM((G * MSG + 8, CP), F32),
            pltpu.VMEM((G, 2, 8, CP), F32),
            pltpu.VMEM((2, HP + 8, CP), F32),
            pltpu.VMEM((KG, 2 * C, PP), BF16),
            pltpu.VMEM((2 * C, 2 * C), BF16),
            pltpu.VMEM((2 * C, 2 * C), BF16),
            pltpu.VMEM((2 * C, 2 * C), BF16),
            pltpu.VMEM((2 * C, 2 * C), BF16),
            pltpu.VMEM((2 * C, PP), F32),
            pltpu.VMEM((2 * C, PP), F32),
            pltpu.VMEM((2 * C, 2 * C), F32),
            pltpu.VMEM((2 * C, 2 * C), F32),
            pltpu.VMEM((2 * C, CP), F32),
            pltpu.VMEM((2 * C, CP), F32),
            pltpu.VMEM((8, 2, 32, CP), F32),
            pltpu.VMEM((8, 2, 32, CP), F32),
            pltpu.VMEM((4, 2, 8, CP), F32),
            pltpu.VMEM((4, 2, 8, CP), F32),
            pltpu.VMEM((2, 8, CP), F32),
            pltpu.VMEM((8, 8, CP), F32),
            pltpu.VMEM((8, CP), F32),
            pltpu.VMEM((4, 8, CP), F32),
            dma((4,)),
            dma((4,)),
            dma((4,)),
            dma((n, G)),
            dma((n, G)),
            dma((n, G)),
            dma((n, G)),
            dma((8,)),
            dma((8,)),
            dma((4,)),
            dma((4,)),
            dma((8,)),
            dma((8,)),
            dma((4,)),
            dma((4,)),
        ],
        compiler_params=pltpu.CompilerParams(
            collective_id=0, has_side_effects=True, vmem_limit_bytes=52 * 1024 * 1024
        ),
        name="afno_backward",
    )(
        x, y, jnp.asarray(lon_table()), jnp.asarray(lat_table()),
        first_weight[:, 0], first_bias[:, 0], second_weight[:, 0], second_bias[:, 0],
    )
    gw1, gb1, gw2, gb2 = pl.pallas_call(
        emit,
        out_shape=(
            jax.ShapeDtypeStruct((2, 6, 1, C), F32),
            jax.ShapeDtypeStruct((2, 1, 6), F32),
            jax.ShapeDtypeStruct((2, 6, 1, C), F32),
            jax.ShapeDtypeStruct((2, 1, 6), F32),
        ),
        in_specs=[vmem],
        out_specs=(vmem, vmem, vmem, vmem),
        name="emit",
    )(pltpu.with_memory_space_constraint(g, pltpu.VMEM))
    grad_in = jnp.transpose(out, (1, 0, 2))[None]
    gw1, gw2 = [jnp.transpose(v, (0, 2, 1, 3)) for v in (gw1, gw2)]
    return (grad_in, gw1, gb1, gw2, gb2)


def solution(mesh):
    in_specs = (
        P("dp", None, "space", None),
        P("dp", None, None, "space", None),
        P(),
        P(),
        P(),
        P(),
    )
    out_specs = (
        P("dp", None, "space", None),
        P(None, None, "dp", None),
        P(None, None, "dp"),
        P(None, None, "dp", None),
        P(None, None, "dp"),
    )
    return jax.shard_map(
        on_device, mesh=mesh, in_specs=in_specs, out_specs=out_specs, check_vma=False
    )
```
